768 devices in a mesh: row: 24 (over x_lo, z), col: 32 (over x_hi, y, core).
Axes of the slice: x: 4 (x_hi: 2, x_lo: 2; x = x_hi * 2 + x_lo), y: 8, z: 12, core: 2. Of those that a mesh axis runs over, the one named last changes fastest.
Arguments:
- features: bfloat16 [98304, 128], P(('row', 'col')), may hold values from -6 to 6
- deg_scale: bfloat16 [98304], P(('row', 'col')), may hold values from 0.049804688 to 0.5
- weight: bfloat16 [128, 256], replicated, may hold values from -0.5 to 0.5
- cotangent: bfloat16 [98304, 256], P(('row', 'col')), may hold values from -6 to 6
- tile_rows: int32 [24, 32, 48], P('row', 'col'), may hold values from 0 to 15, as said below
- tile_cols: int32 [24, 32, 48], P('row', 'col'), may hold values from 0 to 11, as said below
- tile_count: int32 [24, 32], P('row', 'col'), may hold values from 6 to 48, as said below
- tile_bits: int32 [24, 32, 48, 32, 256], P('row', 'col'), may hold values from 0 to 255, as said below
Outputs:
- activations: bfloat16 [98304, 256], P(('row', 'col'))
- input_grad: bfloat16 [98304, 128], P(('row', 'col'))
- weight_grad: float32 [128, 256], replicated
The draws below stay inside these ranges and needn't reach their ends.
Inputs may be any that keep to these rules, and one draw needn't show every extreme that they name: The 48 slots of one block name distinct pairs (tile_rows, tile_cols). `tile_cols`: paired with tile_rows slot by slot. `tile_count`: some block fills all 48 slots. `tile_bits`: bit k of word [a, b] of a slot is the tile's entry in row 8 a + k and column b.
All inputs are finite; a program needn't handle non-finite values.
Results may differ from the reference program's by a relative error of at most 0.0065.
Values may be sent and summed in bfloat16 or wider, within the bound.
A program may use at most 32 MiB of HBM per device.

```python
import math
import jax
import jax.numpy as jnp
from jax import lax

FI = 128
FO = 256
VERT_DEV = 128
TILE = 256
ROW_BLOCKS = 24
COL_BLOCKS = 32
NV = 98304
ROW_TILES = 16
COL_TILES = 12
SLOTS = 48


def tile_positions(key):
    shared_key = jax.random.fold_in(key, 11)
    device_keys = jax.random.split(shared_key, ROW_BLOCKS * COL_BLOCKS)
    positions = ROW_TILES * COL_TILES

    def shuffle(device_key):
        return jax.random.permutation(device_key, positions)[:SLOTS]
    return jax.vmap(shuffle)(device_keys).reshape(ROW_BLOCKS, COL_BLOCKS, SLOTS).astype(jnp.int32)


def draw_tile_rows(key, part):
    shared = tile_positions(key)
    return (shared // COL_TILES).astype(jnp.int32)


def draw_tile_cols(key, part):
    shared = tile_positions(key)
    return (shared % COL_TILES).astype(jnp.int32)


def draw_tile_count(key, part):
    key = jax.random.fold_in(key, 5)
    first, second = jax.random.split(key)
    levels = jax.random.randint(first, (ROW_BLOCKS * COL_BLOCKS,), 0, 4).astype(jnp.int32)
    ranking = jax.random.permutation(second, ROW_BLOCKS * COL_BLOCKS)
    levels = levels.at[ranking[0]].set(0).at[ranking[1]].set(3)
    live_counts = jnp.maximum(jnp.right_shift(jnp.full_like(levels, SLOTS), levels), 1)
    return live_counts.reshape(ROW_BLOCKS, COL_BLOCKS).astype(jnp.int32)


def draw_tile_bits(key, part):
    key = jax.random.fold_in(key, 7)
    word_keys = jax.random.split(key, 9)
    word_shape = (ROW_BLOCKS, COL_BLOCKS, SLOTS, TILE // 8, TILE)
    combined = jnp.full(word_shape, 255, jnp.int32)
    for index in range(8):
        random_word = jax.random.randint(word_keys[index], word_shape, 0, 256).astype(jnp.int32)
        combined = jnp.bitwise_and(combined, random_word)
    place_keys = jax.random.split(word_keys[8], 5)
    first_place = jax.random.randint(place_keys[0], (), 0, ROW_BLOCKS).astype(jnp.int32)
    second_place = jax.random.randint(place_keys[1], (), 0, COL_BLOCKS).astype(jnp.int32)
    third_place = jax.random.randint(place_keys[2], (), 0, SLOTS).astype(jnp.int32)
    fourth_place = jax.random.randint(place_keys[3], (), 0, TILE // 8).astype(jnp.int32)
    fifth_place = jax.random.randint(place_keys[4], (), 0, TILE).astype(jnp.int32)
    combined = combined.at[first_place, second_place, third_place, fourth_place, fifth_place].set(255)
    return combined.astype(jnp.int32)


def steps_of(own_key, shape, pieces, low, largest):
    gain, own = 1.0, jax.random.fold_in(own_key, 6)
    for axis_at, blocks in pieces:
        heights = jnp.exp(jax.random.uniform(jax.random.fold_in(own, axis_at), (blocks,), jnp.float32, low / len(pieces), largest / len(pieces)))
        gain = gain * jnp.repeat(heights, shape[axis_at] // blocks).reshape([-1 if axis == axis_at else 1 for axis in range(len(shape))])
    return gain


def centred(key, extent, scale, most, pieces=(), held_as=jnp.bfloat16):
    drawn = scale * jax.random.normal(key, extent, jnp.float32)
    if pieces:
        drawn = drawn * steps_of(key, extent, pieces, -0.22, 0.18)
    return jnp.clip(drawn, -most, most).astype(held_as)


def setup_inputs(seed: int = 0) -> dict:
    key_list = jax.random.split(jax.random.key(seed), 9)
    return {
        "features": centred(key_list[0], (NV, FI), 1.0, 6.0, ((0, 768),)),
        "deg_scale": jnp.clip(jnp.exp(math.log(0.5) - 2.306499 * jax.random.uniform(key_list[1], (NV,), jnp.float32) ** steps_of(key_list[1], (NV,), ((0, 768),), -0.2, 0.2)), 0.049804688, 0.5).astype(jnp.bfloat16),
        "weight": centred(key_list[2], (FI, FO), FI ** -0.5, 0.5),
        "cotangent": centred(key_list[3], (NV, FO), 1.0, 6.0, ((0, 768),)),
        "tile_rows": draw_tile_rows(jax.random.fold_in(key_list[8], 71), 0),
        "tile_cols": draw_tile_cols(jax.random.fold_in(key_list[8], 71), 0),
        "tile_count": draw_tile_count(jax.random.fold_in(key_list[8], 71), 0),
        "tile_bits": draw_tile_bits(jax.random.fold_in(key_list[8], 71), 0),
    }


def unpack_tiles(packed):
    shifts = jnp.arange(8, dtype=jnp.int32)
    bit_values = jnp.bitwise_and(jnp.right_shift(packed[:, :, None, :], shifts[None, None, :, None]), 1)
    return bit_values.reshape(packed.shape[0], packed.shape[1] * 8, packed.shape[2])

def silu_slope(pre_act):
    sigmoid_value = jax.nn.sigmoid(pre_act)
    return sigmoid_value * (1.0 + pre_act * (1.0 - sigmoid_value))

def reference(features, deg_scale, weight, cotangent, tile_rows, tile_cols, tile_count, tile_bits):
    scale = deg_scale.astype(jnp.float32)
    scaled = (features.astype(jnp.float32) * scale[:, None]).astype(jnp.bfloat16)
    grid = scaled.reshape(ROW_BLOCKS, COL_BLOCKS, VERT_DEV, FI)
    slot_ids = jnp.arange(SLOTS, dtype=jnp.int32)

    def forward_block(row_pos):

        def block_step(running, col_pos):
            source = grid[:, col_pos].reshape(COL_TILES, TILE, FI)
            mask_tiles = unpack_tiles(tile_bits[row_pos, col_pos]).astype(jnp.float32)
            picked = source[tile_cols[row_pos, col_pos]].astype(jnp.float32)
            products = jnp.einsum('sab,sbf->saf', mask_tiles, picked)
            live_slots = (slot_ids < tile_count[row_pos, col_pos]).astype(jnp.float32)
            running = running.at[tile_rows[row_pos, col_pos]].add(products * live_slots[:, None, None])
            return (running, None)
        initial = jnp.zeros((ROW_TILES, TILE, FI), jnp.float32)
        running, _ = lax.scan(block_step, initial, jnp.arange(COL_BLOCKS, dtype=jnp.int32))
        return running.reshape(COL_BLOCKS * VERT_DEV, FI)
    summed = lax.map(forward_block, jnp.arange(ROW_BLOCKS, dtype=jnp.int32)).reshape(NV, FI)
    hidden = (summed * scale[:, None]).astype(jnp.bfloat16)
    pre_act = jnp.dot(hidden, weight, preferred_element_type=jnp.float32)
    activations = jax.nn.silu(pre_act).astype(jnp.bfloat16)
    slope_term = (cotangent.astype(jnp.float32) * silu_slope(pre_act)).astype(jnp.bfloat16)
    weight_grad = jnp.dot(hidden.T, slope_term, preferred_element_type=jnp.float32) / math.sqrt(NV)
    spread = jnp.dot(slope_term, weight.T, preferred_element_type=jnp.float32)
    back = (spread * scale[:, None]).astype(jnp.bfloat16)
    back_grid = back.reshape(ROW_BLOCKS, COL_BLOCKS * VERT_DEV, FI)

    def backward_block(col_pos):

        def block_step(running, row_pos):
            source = back_grid[row_pos].reshape(ROW_TILES, TILE, FI)
            mask_tiles = unpack_tiles(tile_bits[row_pos, col_pos]).astype(jnp.float32)
            picked = source[tile_rows[row_pos, col_pos]].astype(jnp.float32)
            products = jnp.einsum('sab,saf->sbf', mask_tiles, picked)
            live_slots = (slot_ids < tile_count[row_pos, col_pos]).astype(jnp.float32)
            running = running.at[tile_cols[row_pos, col_pos]].add(products * live_slots[:, None, None])
            return (running, None)
        initial = jnp.zeros((COL_TILES, TILE, FI), jnp.float32)
        running, _ = lax.scan(block_step, initial, jnp.arange(ROW_BLOCKS, dtype=jnp.int32))
        return running.reshape(ROW_BLOCKS, VERT_DEV, FI)
    column_parts = lax.map(backward_block, jnp.arange(COL_BLOCKS, dtype=jnp.int32))
    gathered = jnp.transpose(column_parts, (1, 0, 2, 3)).reshape(NV, FI)
    input_grad = (gathered * scale[:, None]).astype(jnp.bfloat16)
    return (activations, input_grad, weight_grad)
```

```python
import functools
import math

import jax
import jax.numpy as jnp
from jax import lax
from jax.experimental import pallas as pl
from jax.experimental.pallas import tpu as pltpu
from jax.sharding import PartitionSpec as P

MESH = pl.DeviceIdType.MESH
F32, BF16 = jnp.float32, jnp.bfloat16
X_LO, Z = 2, 12
X_HI, Y, CORES = 2, 8, 2
V = 128
VMEM_BYTES = 40 * 1024 * 1024
WHOLE = pl.BlockSpec(memory_space=pltpu.VMEM)
SCALARS = pl.BlockSpec(memory_space=pltpu.SMEM)


class Place:
    def __init__(self):
        row, col = lax.axis_index("row"), lax.axis_index("col")
        self.row, self.col = row, col
        self.x_lo, self.z = row // Z, row % Z
        self.x_hi, self.y, self.core = col // (Y * CORES), (col // CORES) % Y, col % CORES

    def at(self, x_lo=None, z=None, x_hi=None, y=None, core=None):
        x_lo = self.x_lo if x_lo is None else x_lo
        z = self.z if z is None else z
        x_hi = self.x_hi if x_hi is None else x_hi
        y = self.y if y is None else y
        core = self.core if core is None else core
        return (x_lo * Z + z, (x_hi * Y + y) * CORES + core)


def greet(peers):
    barrier = pltpu.get_barrier_semaphore()
    for peer in peers:
        pl.semaphore_signal(barrier, inc=1, device_id=peer, device_id_type=MESH)
    return lambda: pl.semaphore_wait(barrier, len(peers))


class Wire:
    def __init__(self, send, recv):
        self.send, self.recv, self.used, self.sent = send, recv, 0, []

    def slot(self):
        self.used += 1
        return self.used - 1

    def copy(self, slot, src, dst, to):
        return pltpu.make_async_remote_copy(
            src_ref=src, dst_ref=dst, send_sem=self.send.at[slot], recv_sem=self.recv.at[slot],
            device_id=to, device_id_type=MESH)

    def start(self, slot, src, dst, to):
        copy = self.copy(slot, src, dst, to)
        copy.start()
        self.sent.append(copy)

    def arrived(self, slot, dst, to):
        self.copy(slot, dst, dst, to).wait_recv()

    def finish(self):
        for copy in self.sent:
            copy.wait_send()


def ring_gather(wire, block, pair, pos, n, right, left, partner, landed=None):
    steps = {"right": n // 2, "left": (n - 1) // 2}
    to = {"right": right, "left": left}
    ways = ("right", "left")
    pair_slot = wire.slot()
    slots = {(w, s, p): wire.slot() for w in ways for s in range(steps[w]) for p in (0, 1)}
    which = (pair, 1 - pair)

    def spot(way, step, p):
        shift = step if way == "left" else n - step
        return block(which[p], (pos + shift) % n)

    def tell(way, step, p):
        if landed is not None:
            shift = step if way == "left" else n - step
            landed(which[p], (pos + shift) % n)

    own = block(pair, pos)
    wire.start(pair_slot, own, own, partner)
    for way in ways:
        wire.start(slots[way, 0, 0], own, own, to[way])
    tell("left", 0, 0)
    other = block(1 - pair, pos)
    wire.arrived(pair_slot, other, partner)
    for way in ways:
        wire.start(slots[way, 0, 1], other, other, to[way])
    tell("left", 0, 1)
    yield
    for step in range(1, max(steps.values()) + 1):
        for p in (0, 1):
            here = []
            for way in ways:
                if step <= steps[way]:
                    ref = spot(way, step, p)
                    wire.arrived(slots[way, step - 1, p], ref, to[way])
                    if step < steps[way]:
                        wire.start(slots[way, step, p], ref, ref, to[way])
                    here.append(way)
            for way in here:
                tell(way, step, p)
        yield


def ring_reduce(wire, value, pair, pos, n, right, left, partner, arms, pair_buf, done):
    steps = {"right": n // 2, "left": (n - 1) // 2}
    to = {"right": right, "left": left}
    ways = ("right", "left")
    slots = {(w, s, p): wire.slot() for w in ways for s in range(steps[w]) for p in (0, 1)}
    pair_slot = wire.slot()
    which = (1 - pair, pair)
    arm = lambda way, step, p: arms.at[ways.index(way), step, p]
    stage = arms.at[2]
    for step in range(max(steps.values())):
        for p in (0, 1):
            for way in ways:
                if step >= steps[way]:
                    continue
                far = steps[way] - step
                target = (pos + (far if way == "right" else n - far)) % n
                total = value(which[p], target)
                if step == 0:
                    src = stage.at[ways.index(way), p]
                else:
                    src = arm(way, step - 1, p)
                    wire.arrived(slots[way, step - 1, p], src, to[way])
                    total = total + src[...].astype(F32)
                src[...] = total.astype(BF16)
                wire.start(slots[way, step, p], src, arm(way, step, p), to[way])
        yield
    totals = []
    for p in (0, 1):
        total = value(which[p], pos)
        for way in ways:
            last = arm(way, steps[way] - 1, p)
            wire.arrived(slots[way, steps[way] - 1, p], last, to[way])
            total = total + last[...].astype(F32)
        totals.append(total)
        if p == 0:
            pair_buf[0] = total.astype(BF16)
            wire.start(pair_slot, pair_buf.at[0], pair_buf.at[1], partner)
    yield
    wire.arrived(pair_slot, pair_buf.at[1], partner)
    done(totals[1] + pair_buf[1].astype(F32))


def together(*jobs):
    jobs = list(jobs)
    while jobs:
        for job in list(jobs):
            try:
                next(job)
            except StopIteration:
                jobs.remove(job)


def column_of(row_vector):
    return jnp.transpose(jnp.broadcast_to(row_vector, (V, V)))


def gather_kernel(features, scale, out, send, recv):
    me = Place()
    right, left = me.at(z=(me.z + 1) % Z), me.at(z=(me.z + Z - 1) % Z)
    partner = me.at(x_lo=1 - me.x_lo)
    ready = greet((right, left, partner))
    scaled = features[...].astype(F32) * column_of(scale[...].astype(F32))
    out[me.row] = scaled.astype(BF16)
    ready()
    wire = Wire(send, recv)
    together(ring_gather(
        wire, lambda pair, pos: out.at[pair * Z + pos], me.x_lo, me.z, Z, right, left, partner))
    wire.finish()


def unpack(words):
    parts = []
    for half in (0, 1):
        part = words[16 * half:16 * half + 16]
        for k in range(8):
            parts.append(jnp.bitwise_and(jnp.right_shift(part, k), 1).astype(F32).astype(BF16))
    return jnp.concatenate(parts, axis=0)


UNROLL = 4


def live_tiles(count, bits, body):
    live = count[0]

    def turn(step, _):
        for u in range(UNROLL):
            slot = step * UNROLL + u
            words = jnp.where(slot < live, bits[slot], 0)
            body(slot, unpack(words))
        return 0

    lax.fori_loop(0, (live + UNROLL - 1) // UNROLL, turn, 0)


def forward_kernel(rows, cols, count, source, bits, out, acc):
    acc[...] = jnp.zeros_like(acc)

    def body(slot, mask):
        i = rows[slot]
        acc[i] = acc[i] + jnp.dot(mask, source[cols[slot]], preferred_element_type=F32)

    live_tiles(count, bits, body)
    for i in range(acc.shape[0]):
        for half in (0, 1):
            out[half, i % Y, i // Y] = acc[i, half * V:half * V + V, :].astype(BF16)


def backward_kernel(rows, cols, count, source, bits, act_in, out, act_out, acc):
    acc[...] = jnp.zeros_like(acc)
    act_out[...] = act_in[...]

    def body(slot, mask):
        i, j = rows[slot], cols[slot]
        y, x_hi = i % Y, i // Y
        back = jnp.concatenate([source[0, y, x_hi], source[1, y, x_hi]], axis=1)
        acc[j] = acc[j] + jnp.dot(back, mask, preferred_element_type=F32)

    live_tiles(count, bits, body)
    for j in range(acc.shape[0]):
        for half in (0, 1):
            out[2 * j + half] = acc[j, :, half * V:half * V + V].astype(BF16)


def vertex_kernel(partial, scale, weight, cotangent, act, row_block, piece,
                  core_buf, arms, pair_buf, natural, slope_buf, grad, grad_core, grad_mine, grad_y,
                  grad_x, send, recv):
    me = Place()
    right, left = me.at(y=(me.y + 1) % Y), me.at(y=(me.y + Y - 1) % Y)
    partner, sibling = me.at(x_hi=1 - me.x_hi), me.at(core=1 - me.core)
    y_peers = [me.at(y=(me.y + d) % Y) for d in range(1, Y)]
    ready = greet([partner, sibling] + y_peers)
    wire = Wire(send, recv)

    order = [4, 5, 3, 6, 2, 7, 1, 0]
    core_slots = {d: wire.slot() for d in order}
    ready()
    for d in order:
        t = (me.y + d) % Y
        wire.start(core_slots[d], partial.at[1 - me.core, t], core_buf.at[t], sibling)
    known = set()

    def value_at(distance):
        def value(pair, pos):
            if distance not in known:
                known.add(distance)
                wire.arrived(core_slots[distance], core_buf.at[pos], sibling)
            return partial[me.core, pos, pair].astype(F32) + core_buf[pos, pair].astype(F32)
        return value

    counter = {"calls": 0}
    plan = []
    for step in range(Y // 2):
        for p in (0, 1):
            plan.append(Y // 2 - step)
            if step < (Y - 1) // 2:
                plan.append(Y - ((Y - 1) // 2 - step))
    plan += [0, 0]

    def value(pair, pos):
        distance = plan[counter["calls"]]
        counter["calls"] += 1
        return value_at(distance)(pair, pos)

    scale_row = scale[...].astype(F32)
    scale_col = column_of(scale_row)
    pieces = []
    together(ring_reduce(wire, value, me.x_hi, me.y, Y, right, left, partner, arms, pair_buf,
                         pieces.append))
    summed = pieces[0]
    for k in range(8):
        natural[pl.ds(k, 16, stride=8), :] = summed[16 * k:16 * k + 16]
    hidden = (natural[...] * scale_col).astype(BF16)
    pre_act = jnp.dot(hidden, weight[...], preferred_element_type=F32)
    sigmoid = 1.0 / (1.0 + jnp.exp(-pre_act))
    slope = sigmoid * (1.0 + pre_act * (1.0 - sigmoid))
    slope_term = (cotangent[...].astype(F32) * slope).astype(BF16)
    back = lax.dot_general(weight[...], slope_term, (((1,), (1,)), ((), ())),
                           preferred_element_type=F32)
    back = (back * scale_row).astype(BF16)
    from_v = lax.broadcasted_iota(jnp.int32, (V, V), 0)
    to_v = lax.broadcasted_iota(jnp.int32, (V, V), 1)
    swap = (from_v == 8 * (to_v % 16) + to_v // 16).astype(F32).astype(BF16)
    row_block[me.core, me.y, me.x_hi] = jnp.dot(
        back, swap, preferred_element_type=F32).astype(BF16)

    forwarded = []

    def forward(pair, pos):
        slot = wire.slot()
        wire.start(slot, row_block.at[me.core, pos, pair], row_block.at[me.core, pos, pair], sibling)
        forwarded.append((slot, row_block.at[1 - me.core, pos, pair]))

    def weight_part():
        act[...] = (pre_act * sigmoid).astype(BF16)
        grad[...] = lax.dot_general(hidden, slope_term, (((0,), (0,)), ((), ())),
                                    preferred_element_type=F32).reshape(2, V // 2, 2 * V)
        slot = wire.slot()
        wire.start(slot, grad.at[1 - me.core], grad_core, sibling)
        yield
        wire.arrived(slot, grad_core, sibling)
        grad_mine[...] = (grad[me.core] + grad_core[...]).reshape(Y, V // 16, 2 * V)
        slots = [wire.slot() for _ in y_peers]
        for d, peer in enumerate(y_peers, 1):
            wire.start(slots[d - 1], grad_mine.at[(me.y + d) % Y], grad_y.at[me.y], peer)
        grad_y[me.y] = grad_mine[me.y]
        yield
        for d, peer in enumerate(y_peers, 1):
            wire.arrived(slots[d - 1], grad_y.at[(me.y + Y - d) % Y], peer)
        total = grad_y[0]
        for k in range(1, Y):
            total = total + grad_y[k]
        grad_x[0] = total[:, :V]
        grad_x[1] = total[:, V:]
        slot = wire.slot()
        wire.start(slot, grad_x.at[1 - me.x_hi], grad_x.at[2], partner)
        yield
        wire.arrived(slot, grad_x.at[2], partner)
        piece[...] = grad_x[me.x_hi] + grad_x[2]

    together(
        ring_gather(wire, lambda pair, pos: row_block.at[me.core, pos, pair], me.x_hi, me.y, Y,
                    right, left, partner, forward),
        weight_part())
    for slot, ref in forwarded:
        wire.arrived(slot, ref, sibling)
    wire.finish()


def scatter_kernel(partial, scale, piece, grad_in, weight_grad, arms, pair_buf, lo_buf, z_buf,
                   send, recv):
    me = Place()
    right, left = me.at(z=(me.z + 1) % Z), me.at(z=(me.z + Z - 1) % Z)
    partner, sibling = me.at(x_lo=1 - me.x_lo), me.at(core=1 - me.core)
    x_peer = me.at(x_hi=1 - me.x_hi)
    z_peers = [me.at(z=(me.z + d) % Z) for d in range(1, Z)]
    y_peers = [me.at(y=(me.y + d) % Y) for d in range(1, Y)]
    ready = greet([partner, sibling, x_peer] + z_peers + y_peers)
    wire = Wire(send, recv)
    scale_row = scale[...].astype(F32)
    ready()

    def value(pair, pos):
        return partial[pair * Z + pos].astype(F32)

    def done(total):
        grad_in[...] = jnp.transpose(total * scale_row).astype(BF16)

    def weight_part():
        slot = wire.slot()
        wire.start(slot, piece, lo_buf, partner)
        yield
        wire.arrived(slot, lo_buf, partner)
        z_buf[me.z] = piece[...] + lo_buf[...]
        slots = [wire.slot() for _ in z_peers]
        for d, peer in enumerate(z_peers, 1):
            wire.start(slots[d - 1], z_buf.at[me.z], z_buf.at[me.z], peer)
        yield
        yield
        for d, peer in enumerate(z_peers, 1):
            wire.arrived(slots[d - 1], z_buf.at[(me.z + Z - d) % Z], peer)
        total = z_buf[0]
        for k in range(1, Z):
            total = total + z_buf[k]
        spot = weight_grad.at[me.core, me.y, me.x_hi]
        spot[...] = total / math.sqrt(X_LO * Z * X_HI * Y * CORES * V)
        slot = wire.slot()
        wire.start(slot, spot, spot, x_peer)
        yield
        wire.arrived(slot, weight_grad.at[me.core, me.y, 1 - me.x_hi], x_peer)
        both = weight_grad.at[me.core, me.y]
        slots = [wire.slot() for _ in y_peers]
        for d, peer in enumerate(y_peers, 1):
            wire.start(slots[d - 1], both, both, peer)
        yield
        for d, peer in enumerate(y_peers, 1):
            wire.arrived(slots[d - 1], weight_grad.at[me.core, (me.y + Y - d) % Y], peer)
        slot = wire.slot()
        wire.start(slot, weight_grad.at[me.core], weight_grad.at[me.core], sibling)
        yield
        wire.arrived(slot, weight_grad.at[1 - me.core], sibling)

    together(
        ring_reduce(wire, value, me.x_lo, me.z, Z, right, left, partner, arms, pair_buf, done),
        weight_part())
    wire.finish()


def sems(count):
    return [pltpu.SemaphoreType.DMA((count,)), pltpu.SemaphoreType.DMA((count,))]


def shape(extent, dtype):
    return jax.ShapeDtypeStruct(extent, dtype)


def talking(collective_id):
    return pltpu.CompilerParams(
        collective_id=collective_id, has_side_effects=True, vmem_limit_bytes=VMEM_BYTES)


def gather_call(features, scale):
    return pl.pallas_call(
        gather_kernel,
        out_shape=shape((X_LO * Z, V, V), BF16),
        in_specs=[WHOLE] * 2,
        out_specs=WHOLE,
        scratch_shapes=sems(2 * Z),
        compiler_params=talking(0),
        name="gather_rows",
    )(features, scale)


def forward_call(rows, cols, count, source, bits):
    return pl.pallas_call(
        forward_kernel,
        out_shape=shape((CORES, Y, X_HI, V, V), BF16),
        in_specs=[SCALARS] * 3 + [WHOLE] * 2,
        out_specs=WHOLE,
        scratch_shapes=[pltpu.VMEM((X_HI * Y, 2 * V, V), F32)],
        compiler_params=pltpu.CompilerParams(vmem_limit_bytes=VMEM_BYTES),
        name="forward_tiles",
    )(rows, cols, count, source, bits)


def vertex_call(partial, scale, weight, cotangent):
    return pl.pallas_call(
        vertex_kernel,
        out_shape=(shape((V, 2 * V), BF16), shape((CORES, Y, X_HI, V, V), BF16), shape((8, V), F32)),
        in_specs=[WHOLE] * 4,
        out_specs=(WHOLE,) * 3,
        scratch_shapes=[
            pltpu.VMEM((Y, X_HI, V, V), BF16),
            pltpu.VMEM((3, Y // 2, 2, V, V), BF16),
            pltpu.VMEM((2, V, V), BF16),
            pltpu.VMEM((V, V), F32),
            pltpu.VMEM((V, 2 * V), BF16),
            pltpu.VMEM((2, V // 2, 2 * V), F32),
            pltpu.VMEM((V // 2, 2 * V), F32),
            pltpu.VMEM((Y, 8, 2 * V), F32),
            pltpu.VMEM((Y, 8, 2 * V), F32),
            pltpu.VMEM((3, 8, V), F32),
        ] + sems(64),
        compiler_params=talking(1),
        name="vertex_part",
    )(partial, scale, weight, cotangent)


def backward_call(rows, cols, count, source, bits, act):
    return pl.pallas_call(
        backward_kernel,
        out_shape=(shape((X_LO * Z, V, V), BF16), shape(act.shape, act.dtype)),
        in_specs=[SCALARS] * 3 + [WHOLE] * 3,
        out_specs=(WHOLE,) * 2,
        scratch_shapes=[pltpu.VMEM((X_LO * Z // 2, V, 2 * V), F32)],
        compiler_params=pltpu.CompilerParams(vmem_limit_bytes=VMEM_BYTES),
        name="backward_tiles",
    )(rows, cols, count, source, bits, act)


def scatter_call(partial, scale, piece):
    return pl.pallas_call(
        scatter_kernel,
        out_shape=(shape((V, V), BF16), shape((CORES, Y, X_HI, 8, V), F32)),
        in_specs=[WHOLE] * 3,
        out_specs=(WHOLE,) * 2,
        scratch_shapes=[
            pltpu.VMEM((3, Z // 2, 2, V, V), BF16),
            pltpu.VMEM((2, V, V), BF16),
            pltpu.VMEM((8, V), F32),
            pltpu.VMEM((Z, 8, V), F32),
        ] + sems(56),
        compiler_params=talking(2),
        name="scatter_rows",
    )(partial, scale, piece)


def on_device(features, deg_scale, weight, cotangent, tile_rows, tile_cols, tile_count, tile_bits):
    rows, cols, count, bits = tile_rows[0, 0], tile_cols[0, 0], tile_count[0], tile_bits[0, 0]
    scale = deg_scale.reshape(1, V)
    column_block = gather_call(features, scale)
    partial = forward_call(rows, cols, count, column_block.reshape(Z, 2 * V, V), bits)
    act, row_block, piece = vertex_call(partial, scale, weight, cotangent)
    partial_back, activations = backward_call(rows, cols, count, row_block, bits, act)
    input_grad, grad = scatter_call(partial_back, scale, piece)
    weight_grad = jnp.transpose(grad, (0, 1, 3, 2, 4)).reshape(V, 2 * V)
    return (activations, input_grad, weight_grad)


def solution(mesh):
    in_specs = (
        P(("row", "col"), None),
        P(("row", "col")),
        P(),
        P(("row", "col"), None),
        P("row", "col", None),
        P("row", "col", None),
        P("row", "col"),
        P("row", "col", None, None, None),
    )
    out_specs = (P(("row", "col"), None), P(("row", "col"), None), P())
    return jax.shard_map(
        on_device, mesh=mesh, in_specs=in_specs, out_specs=out_specs, check_vma=False)
```

```python
import functools
import math

import jax
import jax.numpy as jnp
from jax import lax
from jax.experimental import pallas as pl
from jax.experimental.pallas import tpu as pltpu
from jax.sharding import PartitionSpec as P

MESH = pl.DeviceIdType.MESH
F32, BF16 = jnp.float32, jnp.bfloat16
X_LO, Z = 2, 12
X_HI, Y, CORES = 2, 8, 2
V = 128
VMEM_BYTES = 40 * 1024 * 1024
WHOLE = pl.BlockSpec(memory_space=pltpu.VMEM)
SCALARS = pl.BlockSpec(memory_space=pltpu.SMEM)


class Place:
    def __init__(self):
        row, col = lax.axis_index("row"), lax.axis_index("col")
        self.row, self.col = row, col
        self.x_lo, self.z = row // Z, row % Z
        self.x_hi, self.y, self.core = col // (Y * CORES), (col // CORES) % Y, col % CORES

    def at(self, x_lo=None, z=None, x_hi=None, y=None, core=None):
        x_lo = self.x_lo if x_lo is None else x_lo
        z = self.z if z is None else z
        x_hi = self.x_hi if x_hi is None else x_hi
        y = self.y if y is None else y
        core = self.core if core is None else core
        return (x_lo * Z + z, (x_hi * Y + y) * CORES + core)


def greet(peers):
    barrier = pltpu.get_barrier_semaphore()
    for peer in peers:
        pl.semaphore_signal(barrier, inc=1, device_id=peer, device_id_type=MESH)
    return lambda: pl.semaphore_wait(barrier, len(peers))


class Wire:
    def __init__(self, send, recv):
        self.send, self.recv, self.used, self.sent = send, recv, 0, []

    def slot(self):
        self.used += 1
        return self.used - 1

    def copy(self, slot, src, dst, to):
        return pltpu.make_async_remote_copy(
            src_ref=src, dst_ref=dst, send_sem=self.send.at[slot], recv_sem=self.recv.at[slot],
            device_id=to, device_id_type=MESH)

    def start(self, slot, src, dst, to):
        copy = self.copy(slot, src, dst, to)
        copy.start()
        self.sent.append(copy)

    def arrived(self, slot, dst, to):
        self.copy(slot, dst, dst, to).wait_recv()

    def finish(self):
        for copy in self.sent:
            copy.wait_send()


def row_gather(wire, me, out):
    def block(offset, pair=None):
        return out.at[(me.x_lo if pair is None else pair) * Z + (me.z + offset) % Z]

    def to(offset):
        return me.at(z=(me.z + offset) % Z)

    partner = me.at(x_lo=1 - me.x_lo)
    near = {o: wire.slot() for o in (3, 9, 2, 10, 1, 11)}
    far = {o: wire.slot() for o in (3, 9, 2, 10, 1, 11)}
    cross = {o: wire.slot() for o in range(Z)}

    def hand_over(offset):
        wire.start(cross[offset], block(offset), block(offset), partner)

    for o in near:
        wire.start(near[o], block(0), block(0), to(o))
    hand_over(0)
    yield
    for o in near:
        source = Z - o
        wire.arrived(near[o], block(source), to(o))
        if o in (3, 9):
            sign = 1 if o == 3 else -1
            half = block(source).at[pl.ds(0 if o == 3 else V // 2, V // 2)]
            wire.start(far[o], half, half, to(3 * sign % Z))
            wire.start(far[2 * sign % Z], block(source), block(source), to(2 * sign % Z))
            wire.start(far[sign % Z], block(source), block(source), to(sign % Z))
        hand_over(source)
    yield
    for o, source in ((1, 8), (11, 4), (2, 7), (10, 5)):
        wire.arrived(far[o], block(source), to(o))
        hand_over(source)
    wire.arrived(far[3], block(6).at[pl.ds(0, V // 2)], to(3))
    wire.arrived(far[9], block(6).at[pl.ds(V // 2, V // 2)], to(9))
    hand_over(6)
    yield
    for o in range(Z):
        wire.arrived(cross[o], block(o, 1 - me.x_lo), partner)


def row_reduce(wire, me, partial, cross_buf, ready, relay, final, done):
    def to(offset):
        return me.at(z=(me.z + offset) % Z)

    partner = me.at(x_lo=1 - me.x_lo)
    order = (4, 8, 5, 7, 6, 2, 10, 1, 11, 3, 9, 0)
    cross = {o: wire.slot() for o in order}
    for o in order:
        t = (me.z + o) % Z
        wire.start(cross[o], partial.at[(1 - me.x_lo) * Z + t], cross_buf.at[t], partner)

    def value(offset):
        t = (me.z + offset) % Z
        wire.arrived(cross[offset], cross_buf.at[t], partner)
        return partial[me.x_lo * Z + t].astype(F32) + cross_buf[t].astype(F32)

    yield
    relayed = {o: wire.slot() for o in (1, 11, 2, 10, 3, 9)}
    relay_at = {1: 0, 11: 1, 2: 2, 10: 3, 3: 4, 9: 5}
    low, high = pl.ds(0, V // 2), pl.ds(V // 2, V // 2)
    for o, hop in ((4, 1), (8, 11), (5, 2), (7, 10)):
        ready[o] = value(o).astype(BF16)
        wire.start(relayed[hop], ready.at[o], relay.at[relay_at[hop]], to(hop))
    ready[6] = value(6).astype(BF16)
    for hop, half in ((3, low), (9, high)):
        wire.start(relayed[hop], ready.at[6, half], relay.at[relay_at[hop], half], to(hop))
    yield
    direct = {o: wire.slot() for o in (2, 10, 1, 11, 3, 9)}
    for o in (2, 10, 1, 11):
        ready[o] = value(o).astype(BF16)
        wire.start(direct[o], ready.at[o], final.at[relay_at[o]], to(o))
    yield
    for o, hops, half, rest in ((3, (1, 2, 3), low, high), (9, (11, 10, 9), high, low)):
        total = value(o)
        for hop in hops[:2]:
            wire.arrived(relayed[hop], relay.at[relay_at[hop]], to(hop))
            total = total + relay[relay_at[hop]].astype(F32)
        last = relay.at[relay_at[hops[2]], half]
        wire.arrived(relayed[hops[2]], last, to(hops[2]))
        cut = V // 2
        top, bottom = total[:cut], total[cut:]
        if o == 3:
            top = top + last[...].astype(F32)
        else:
            bottom = bottom + last[...].astype(F32)
        ready[o, low] = top.astype(BF16)
        ready[o, high] = bottom.astype(BF16)
        wire.start(direct[o], ready.at[o], final.at[relay_at[o]], to(o))
    total = value(0)
    yield
    for o in (2, 10, 1, 11, 3, 9):
        wire.arrived(direct[o], final.at[relay_at[o]], to(o))
        total = total + final[relay_at[o]].astype(F32)
    done(total)


def col_reduce(wire, me, partial, core_buf, cross_out, cross_buf, ready, final, done):
    sibling, partner = me.at(core=1 - me.core), me.at(x_hi=1 - me.x_hi)
    order = (4, 5, 3, 6, 2, 7, 1, 0)
    cores = {o: wire.slot() for o in order}
    cross = {o: wire.slot() for o in order}
    direct = {o: wire.slot() for o in order[:-1]}
    spot = lambda o: (me.y + o) % Y
    for o in order:
        wire.start(cores[o], partial.at[1 - me.core, spot(o)], core_buf.at[spot(o)], sibling)
    for o in order:
        t = spot(o)
        wire.arrived(cores[o], core_buf.at[t], sibling)
        other = partial[me.core, t, 1 - me.x_hi].astype(F32) + core_buf[t, 1 - me.x_hi].astype(F32)
        cross_out[o] = other.astype(BF16)
        wire.start(cross[o], cross_out.at[o], cross_buf.at[t], partner)

    def value(o):
        t = spot(o)
        wire.arrived(cross[o], cross_buf.at[t], partner)
        own = partial[me.core, t, me.x_hi].astype(F32) + core_buf[t, me.x_hi].astype(F32)
        return own + cross_buf[t].astype(F32)

    for o in order[:-1]:
        ready[o] = value(o).astype(BF16)
        wire.start(direct[o], ready.at[o], final.at[o], me.at(y=spot(o)))
    total = value(0)
    for o in order[:-1]:
        wire.arrived(direct[o], final.at[o], me.at(y=spot(o)))
        total = total + final[o].astype(F32)
    done(total)


def col_gather(wire, me, row_block):
    sibling, partner = me.at(core=1 - me.core), me.at(x_hi=1 - me.x_hi)

    def block(offset, x_hi, core=None):
        return row_block.at[me.core if core is None else core, (me.y + offset) % Y, x_hi]

    direct = {o: wire.slot() for o in range(1, Y)}
    cross = {o: wire.slot() for o in range(Y)}
    mine = {o: wire.slot() for o in range(Y)}
    theirs = {o: wire.slot() for o in range(Y)}
    own = block(0, me.x_hi)
    for o in (4, 3, 5, 2, 6, 1, 7):
        wire.start(direct[o], own, own, me.at(y=(me.y + o) % Y))

    def hand_over(o):
        here = block(o, me.x_hi)
        wire.start(cross[o], here, here, partner)
        wire.start(mine[o], here, here, sibling)

    hand_over(0)
    yield
    for o in (3, 5, 2, 6):
        wire.arrived(direct[o], block(Y - o, me.x_hi), me.at(y=(me.y + o) % Y))
        hand_over(Y - o)
    yield
    for o in (1, 7, 4):
        wire.arrived(direct[o], block(Y - o, me.x_hi), me.at(y=(me.y + o) % Y))
        hand_over(Y - o)
    yield
    for o in (0, 5, 3, 6, 2, 7, 1, 4):
        here = block(o, 1 - me.x_hi)
        wire.arrived(cross[o], here, partner)
        wire.start(theirs[o], here, here, sibling)
    yield
    for o in range(Y):
        wire.arrived(mine[o], block(o, me.x_hi, 1 - me.core), sibling)
        wire.arrived(theirs[o], block(o, 1 - me.x_hi, 1 - me.core), sibling)


def together(*jobs):
    jobs = list(jobs)
    while jobs:
        for job in list(jobs):
            try:
                next(job)
            except StopIteration:
                jobs.remove(job)


def column_of(row_vector):
    return jnp.transpose(jnp.broadcast_to(row_vector, (V, V)))


def gather_kernel(features, scale, out, send, recv):
    me = Place()
    peers = [me.at(z=(me.z + d) % Z) for d in (1, 2, 3, 9, 10, 11)]
    ready = greet(peers + [me.at(x_lo=1 - me.x_lo)])
    scaled = features[...].astype(F32) * column_of(scale[...].astype(F32))
    out[me.row] = scaled.astype(BF16)
    ready()
    wire = Wire(send, recv)
    together(row_gather(wire, me, out))
    wire.finish()


def unpack(words):
    parts = []
    for half in (0, 1):
        part = words[16 * half:16 * half + 16]
        for k in range(8):
            parts.append(jnp.bitwise_and(jnp.right_shift(part, k), 1).astype(F32).astype(BF16))
    return jnp.concatenate(parts, axis=0)


UNROLL = 4


def live_tiles(count, bits, body):
    live = count[0]

    def turn(step, _):
        for u in range(UNROLL):
            slot = step * UNROLL + u
            words = jnp.where(slot < live, bits[slot], 0)
            body(slot, unpack(words))
        return 0

    lax.fori_loop(0, (live + UNROLL - 1) // UNROLL, turn, 0)


def forward_kernel(rows, cols, count, source, bits, out, acc):
    acc[...] = jnp.zeros_like(acc)

    def body(slot, mask):
        i = rows[slot]
        acc[i] = acc[i] + jnp.dot(mask, source[cols[slot]], preferred_element_type=F32)

    live_tiles(count, bits, body)
    for i in range(acc.shape[0]):
        for half in (0, 1):
            out[half, i % Y, i // Y] = acc[i, half * V:half * V + V, :].astype(BF16)


def backward_kernel(rows, cols, count, source, bits, act_in, out, act_out, acc):
    acc[...] = jnp.zeros_like(acc)
    act_out[...] = act_in[...]

    def body(slot, mask):
        i, j = rows[slot], cols[slot]
        y, x_hi = i % Y, i // Y
        back = jnp.concatenate([source[0, y, x_hi], source[1, y, x_hi]], axis=1)
        acc[j] = acc[j] + jnp.dot(back, mask, preferred_element_type=F32)

    live_tiles(count, bits, body)
    for j in range(acc.shape[0]):
        for half in (0, 1):
            out[2 * j + half] = acc[j, :, half * V:half * V + V].astype(BF16)


def vertex_kernel(partial, scale, weight, cotangent, act, row_block, piece,
                  core_buf, cross_out, cross_buf, outgoing, final, natural, grad, grad_core, grad_mine,
                  grad_y, grad_x, send, recv):
    me = Place()
    partner, sibling = me.at(x_hi=1 - me.x_hi), me.at(core=1 - me.core)
    y_peers = [me.at(y=(me.y + d) % Y) for d in range(1, Y)]
    ready = greet([partner, sibling] + y_peers)
    wire = Wire(send, recv)
    scale_row = scale[...].astype(F32)
    scale_col = column_of(scale_row)
    ready()
    pieces = []
    col_reduce(wire, me, partial, core_buf, cross_out, cross_buf, outgoing, final, pieces.append)
    summed = pieces[0]
    for k in range(8):
        natural[pl.ds(k, 16, stride=8), :] = summed[16 * k:16 * k + 16]
    hidden = (natural[...] * scale_col).astype(BF16)
    pre_act = jnp.dot(hidden, weight[...], preferred_element_type=F32)
    sigmoid = 1.0 / (1.0 + jnp.exp(-pre_act))
    slope = sigmoid * (1.0 + pre_act * (1.0 - sigmoid))
    slope_term = (cotangent[...].astype(F32) * slope).astype(BF16)
    back = lax.dot_general(weight[...], slope_term, (((1,), (1,)), ((), ())),
                           preferred_element_type=F32)
    back = (back * scale_row).astype(BF16)
    from_v = lax.broadcasted_iota(jnp.int32, (V, V), 0)
    to_v = lax.broadcasted_iota(jnp.int32, (V, V), 1)
    swap = (from_v == 8 * (to_v % 16) + to_v // 16).astype(F32).astype(BF16)
    row_block[me.core, me.y, me.x_hi] = jnp.dot(
        back, swap, preferred_element_type=F32).astype(BF16)

    def weight_part():
        act[...] = (pre_act * sigmoid).astype(BF16)
        grad[...] = lax.dot_general(hidden, slope_term, (((0,), (0,)), ((), ())),
                                    preferred_element_type=F32).reshape(2, V // 2, 2 * V)
        slot = wire.slot()
        wire.start(slot, grad.at[1 - me.core], grad_core, sibling)
        yield
        wire.arrived(slot, grad_core, sibling)
        grad_mine[...] = (grad[me.core] + grad_core[...]).reshape(Y, V // 16, 2 * V)
        slots = [wire.slot() for _ in y_peers]
        for d, peer in enumerate(y_peers, 1):
            wire.start(slots[d - 1], grad_mine.at[(me.y + d) % Y], grad_y.at[me.y], peer)
        grad_y[me.y] = grad_mine[me.y]
        yield
        for d, peer in enumerate(y_peers, 1):
            wire.arrived(slots[d - 1], grad_y.at[(me.y + Y - d) % Y], peer)
        total = grad_y[0]
        for k in range(1, Y):
            total = total + grad_y[k]
        grad_x[0] = total[:, :V]
        grad_x[1] = total[:, V:]
        slot = wire.slot()
        wire.start(slot, grad_x.at[1 - me.x_hi], grad_x.at[2], partner)
        yield
        wire.arrived(slot, grad_x.at[2], partner)
        piece[...] = grad_x[me.x_hi] + grad_x[2]

    together(col_gather(wire, me, row_block), weight_part())
    wire.finish()


def scatter_kernel(partial, scale, piece, grad_in, weight_grad, cross_buf, outgoing, relay, final,
                   lo_buf, z_buf, send, recv):
    me = Place()
    partner, sibling = me.at(x_lo=1 - me.x_lo), me.at(core=1 - me.core)
    x_peer = me.at(x_hi=1 - me.x_hi)
    z_peers = [me.at(z=(me.z + d) % Z) for d in range(1, Z)]
    y_peers = [me.at(y=(me.y + d) % Y) for d in range(1, Y)]
    ready = greet([partner, sibling, x_peer] + z_peers + y_peers)
    wire = Wire(send, recv)
    scale_row = scale[...].astype(F32)
    ready()

    def done(total):
        grad_in[...] = jnp.transpose(total * scale_row).astype(BF16)

    def weight_part():
        slot = wire.slot()
        wire.start(slot, piece, lo_buf, partner)
        yield
        wire.arrived(slot, lo_buf, partner)
        z_buf[me.z] = piece[...] + lo_buf[...]
        slots = [wire.slot() for _ in z_peers]
        for d, peer in enumerate(z_peers, 1):
            wire.start(slots[d - 1], z_buf.at[me.z], z_buf.at[me.z], peer)
        yield
        yield
        for d, peer in enumerate(z_peers, 1):
            wire.arrived(slots[d - 1], z_buf.at[(me.z + Z - d) % Z], peer)
        total = z_buf[0]
        for k in range(1, Z):
            total = total + z_buf[k]
        spot = weight_grad.at[me.core, me.y, me.x_hi]
        spot[...] = total / math.sqrt(X_LO * Z * X_HI * Y * CORES * V)
        slot = wire.slot()
        wire.start(slot, spot, spot, x_peer)
        yield
        wire.arrived(slot, weight_grad.at[me.core, me.y, 1 - me.x_hi], x_peer)
        both = weight_grad.at[me.core, me.y]
        slots = [wire.slot() for _ in y_peers]
        for d, peer in enumerate(y_peers, 1):
            wire.start(slots[d - 1], both, both, peer)
        yield
        for d, peer in enumerate(y_peers, 1):
            wire.arrived(slots[d - 1], weight_grad.at[me.core, (me.y + Y - d) % Y], peer)
        slot = wire.slot()
        wire.start(slot, weight_grad.at[me.core], weight_grad.at[me.core], sibling)
        yield
        wire.arrived(slot, weight_grad.at[1 - me.core], sibling)

    together(
        weight_part(),
        row_reduce(wire, me, partial, cross_buf, outgoing, relay, final, done))
    wire.finish()


def sems(count):
    return [pltpu.SemaphoreType.DMA((count,)), pltpu.SemaphoreType.DMA((count,))]


def shape(extent, dtype):
    return jax.ShapeDtypeStruct(extent, dtype)


def talking(collective_id):
    return pltpu.CompilerParams(
        collective_id=collective_id, has_side_effects=True, vmem_limit_bytes=VMEM_BYTES)


def gather_call(features, scale):
    return pl.pallas_call(
        gather_kernel,
        out_shape=shape((X_LO * Z, V, V), BF16),
        in_specs=[WHOLE] * 2,
        out_specs=WHOLE,
        scratch_shapes=sems(24),
        compiler_params=talking(0),
        name="gather_rows",
    )(features, scale)


def forward_call(rows, cols, count, source, bits):
    return pl.pallas_call(
        forward_kernel,
        out_shape=shape((CORES, Y, X_HI, V, V), BF16),
        in_specs=[SCALARS] * 3 + [WHOLE] * 2,
        out_specs=WHOLE,
        scratch_shapes=[pltpu.VMEM((X_HI * Y, 2 * V, V), F32)],
        compiler_params=pltpu.CompilerParams(vmem_limit_bytes=VMEM_BYTES),
        name="forward_tiles",
    )(rows, cols, count, source, bits)


def vertex_call(partial, scale, weight, cotangent):
    return pl.pallas_call(
        vertex_kernel,
        out_shape=(shape((V, 2 * V), BF16), shape((CORES, Y, X_HI, V, V), BF16), shape((8, V), F32)),
        in_specs=[WHOLE] * 4,
        out_specs=(WHOLE,) * 3,
        scratch_shapes=[
            pltpu.VMEM((Y, X_HI, V, V), BF16),
            pltpu.VMEM((Y, V, V), BF16),
            pltpu.VMEM((Y, V, V), BF16),
            pltpu.VMEM((Y, V, V), BF16),
            pltpu.VMEM((Y, V, V), BF16),
            pltpu.VMEM((V, V), F32),
            pltpu.VMEM((2, V // 2, 2 * V), F32),
            pltpu.VMEM((V // 2, 2 * V), F32),
            pltpu.VMEM((Y, 8, 2 * V), F32),
            pltpu.VMEM((Y, 8, 2 * V), F32),
            pltpu.VMEM((3, 8, V), F32),
        ] + sems(64),
        compiler_params=talking(1),
        name="vertex_part",
    )(partial, scale, weight, cotangent)


def backward_call(rows, cols, count, source, bits, act):
    return pl.pallas_call(
        backward_kernel,
        out_shape=(shape((X_LO * Z, V, V), BF16), shape(act.shape, act.dtype)),
        in_specs=[SCALARS] * 3 + [WHOLE] * 3,
        out_specs=(WHOLE,) * 2,
        scratch_shapes=[pltpu.VMEM((X_LO * Z // 2, V, 2 * V), F32)],
        compiler_params=pltpu.CompilerParams(vmem_limit_bytes=VMEM_BYTES),
        name="backward_tiles",
    )(rows, cols, count, source, bits, act)


def scatter_call(partial, scale, piece):
    return pl.pallas_call(
        scatter_kernel,
        out_shape=(shape((V, V), BF16), shape((CORES, Y, X_HI, 8, V), F32)),
        in_specs=[WHOLE] * 3,
        out_specs=(WHOLE,) * 2,
        scratch_shapes=[
            pltpu.VMEM((Z, V, V), BF16),
            pltpu.VMEM((Z, V, V), BF16),
            pltpu.VMEM((6, V, V), BF16),
            pltpu.VMEM((6, V, V), BF16),
            pltpu.VMEM((8, V), F32),
            pltpu.VMEM((Z, 8, V), F32),
        ] + sems(56),
        compiler_params=talking(2),
        name="scatter_rows",
    )(partial, scale, piece)


def on_device(features, deg_scale, weight, cotangent, tile_rows, tile_cols, tile_count, tile_bits):
    rows, cols, count, bits = tile_rows[0, 0], tile_cols[0, 0], tile_count[0], tile_bits[0, 0]
    scale = deg_scale.reshape(1, V)
    column_block = gather_call(features, scale)
    partial = forward_call(rows, cols, count, column_block.reshape(Z, 2 * V, V), bits)
    act, row_block, piece = vertex_call(partial, scale, weight, cotangent)
    partial_back, activations = backward_call(rows, cols, count, row_block, bits, act)
    input_grad, grad = scatter_call(partial_back, scale, piece)
    weight_grad = jnp.transpose(grad, (0, 1, 3, 2, 4)).reshape(V, 2 * V)
    return (activations, input_grad, weight_grad)


def solution(mesh):
    in_specs = (
        P(("row", "col"), None),
        P(("row", "col")),
        P(),
        P(("row", "col"), None),
        P("row", "col", None),
        P("row", "col", None),
        P("row", "col"),
        P("row", "col", None, None, None),
    )
    out_specs = (P(("row", "col"), None), P(("row", "col"), None), P())
    return jax.shard_map(
        on_device, mesh=mesh, in_specs=in_specs, out_specs=out_specs, check_vma=False)
```

```python
import functools
import math

import jax
import jax.numpy as jnp
from jax import lax
from jax.experimental import pallas as pl
from jax.experimental.pallas import tpu as pltpu
from jax.sharding import PartitionSpec as P

MESH = pl.DeviceIdType.MESH
F32, BF16 = jnp.float32, jnp.bfloat16
X_LO, Z = 2, 12
X_HI, Y, CORES = 2, 8, 2
V = 128
VMEM_BYTES = 24 * 1024 * 1024
WHOLE = pl.BlockSpec(memory_space=pltpu.VMEM)
SCALARS = pl.BlockSpec(memory_space=pltpu.SMEM)


class Place:
    def __init__(self):
        row, col = lax.axis_index("row"), lax.axis_index("col")
        self.row, self.col = row, col
        self.x_lo, self.z = row // Z, row % Z
        self.x_hi, self.y, self.core = col // (Y * CORES), (col // CORES) % Y, col % CORES

    def at(self, x_lo=None, z=None, x_hi=None, y=None, core=None):
        x_lo = self.x_lo if x_lo is None else x_lo
        z = self.z if z is None else z
        x_hi = self.x_hi if x_hi is None else x_hi
        y = self.y if y is None else y
        core = self.core if core is None else core
        return (x_lo * Z + z, (x_hi * Y + y) * CORES + core)


def greet(peers):
    barrier = pltpu.get_barrier_semaphore()
    for peer in peers:
        pl.semaphore_signal(barrier, inc=1, device_id=peer, device_id_type=MESH)
    return lambda: pl.semaphore_wait(barrier, len(peers))


class Wire:
    def __init__(self, send, recv):
        self.send, self.recv, self.used, self.sent = send, recv, 0, []

    def slot(self):
        self.used += 1
        return self.used - 1

    def copy(self, slot, src, dst, to):
        return pltpu.make_async_remote_copy(
            src_ref=src, dst_ref=dst, send_sem=self.send.at[slot], recv_sem=self.recv.at[slot],
            device_id=to, device_id_type=MESH)

    def start(self, slot, src, dst, to):
        copy = self.copy(slot, src, dst, to)
        copy.start()
        self.sent.append(copy)

    def arrived(self, slot, dst, to):
        self.copy(slot, dst, dst, to).wait_recv()

    def finish(self):
        for copy in self.sent:
            copy.wait_send()


def row_gather(wire, me, out):
    def block(offset, pair=me.x_lo):
        return out.at[pair * Z + (me.z + offset) % Z]

    def to(offset):
        return me.at(z=(me.z + offset) % Z)

    partner, other = me.at(x_lo=1 - me.x_lo), 1 - me.x_lo
    near = {o: wire.slot() for o in (3, 9, 2, 10, 1, 11)}
    far = {o: wire.slot() for o in (3, 9, 2, 10, 1, 11)}
    cross = {o: wire.slot() for o in (0, 9, 3, 10, 2, 7, 5, 6)}
    side = {o: wire.slot() for o in (1, 11)}
    side_far = {o: wire.slot() for o in (1, 11)}

    def hand_over(offset):
        wire.start(cross[offset], block(offset), block(offset), partner)

    for o in near:
        wire.start(near[o], block(0), block(0), to(o))
    hand_over(0)
    yield
    wire.arrived(cross[0], block(0, other), partner)
    for o in side:
        wire.start(side[o], block(0, other), block(0, other), to(o))
    for o in near:
        source = Z - o
        wire.arrived(near[o], block(source), to(o))
        if o in (3, 9):
            sign = 1 if o == 3 else -1
            half = block(source).at[pl.ds(0 if o == 3 else V // 2, V // 2)]
            wire.start(far[o], half, half, to(3 * sign % Z))
            wire.start(far[2 * sign % Z], block(source), block(source), to(2 * sign % Z))
            wire.start(far[sign % Z], block(source), block(source), to(sign % Z))
        if o not in side:
            hand_over(source)
    yield
    for o, source in ((1, 9), (11, 3)):
        wire.arrived(cross[source], block(source, other), partner)
        wire.start(side_far[o], block(source, other), block(source, other), to(o))
    for o, source in ((2, 7), (10, 5)):
        wire.arrived(far[o], block(source), to(o))
        hand_over(source)
    wire.arrived(far[3], block(6).at[pl.ds(0, V // 2)], to(3))
    wire.arrived(far[9], block(6).at[pl.ds(V // 2, V // 2)], to(9))
    hand_over(6)
    yield
    for o, source in ((1, 8), (11, 4)):
        wire.arrived(far[o], block(source), to(o))
        wire.arrived(side[o], block(Z - o, other), to(o))
        wire.arrived(side_far[o], block(source, other), to(o))
    for o in (10, 2, 7, 5, 6):
        wire.arrived(cross[o], block(o, other), partner)


def row_reduce(wire, me, partial, cross_buf, ready, relay, final, done):
    def to(offset):
        return me.at(z=(me.z + offset) % Z)

    def term(pair, offset):
        return partial.at[pair * Z + (me.z + offset) % Z]

    partner, other = me.at(x_lo=1 - me.x_lo), 1 - me.x_lo
    order = (4, 8, 5, 7, 6, 3, 9, 2, 10)
    cross = {o: wire.slot() for o in order + (0,)}
    direct = {o: wire.slot() for o in (2, 10, 1, 11, 3, 9)}
    side = {o: wire.slot() for o in (1, 11)}
    relay_at = {1: 0, 11: 1, 2: 2, 10: 3, 3: 4, 9: 5}
    side_at = {1: 6, 11: 7}
    for o in order:
        wire.start(cross[o], term(other, o), cross_buf.at[(me.z + o) % Z], partner)
    for o in (1, 11):
        wire.start(side[o], term(other, o), relay.at[side_at[o]], to(o))
        wire.start(direct[o], term(me.x_lo, o), final.at[relay_at[o]], to(o))

    def value(offset):
        t = (me.z + offset) % Z
        wire.arrived(cross[offset], cross_buf.at[t], partner)
        return term(me.x_lo, offset)[...].astype(F32) + cross_buf[t].astype(F32)

    yield
    relayed = {o: wire.slot() for o in (1, 11, 2, 10, 3, 9)}
    low, high = pl.ds(0, V // 2), pl.ds(V // 2, V // 2)
    for o, hop in ((4, 1), (8, 11), (5, 2), (7, 10)):
        ready[o] = value(o).astype(BF16)
        wire.start(relayed[hop], ready.at[o], relay.at[relay_at[hop]], to(hop))
    ready[6] = value(6).astype(BF16)
    for hop, half in ((3, low), (9, high)):
        wire.start(relayed[hop], ready.at[6, half], relay.at[relay_at[hop], half], to(hop))
    total = term(other, 0)[...].astype(F32)
    for o in (1, 11):
        wire.arrived(side[o], relay.at[side_at[o]], to(o))
        total = total + relay[side_at[o]].astype(F32)
    ready[0] = total.astype(BF16)
    wire.start(cross[0], ready.at[0], cross_buf.at[me.z], partner)
    yield
    sums = {o: value(o) for o in (3, 9)}
    for o in (2, 10):
        ready[o] = value(o).astype(BF16)
        wire.start(direct[o], ready.at[o], final.at[relay_at[o]], to(o))
    yield
    for o, hops, half in ((3, (1, 2, 3), low), (9, (11, 10, 9), high)):
        total = sums[o]
        for hop in hops[:2]:
            wire.arrived(relayed[hop], relay.at[relay_at[hop]], to(hop))
            total = total + relay[relay_at[hop]].astype(F32)
        last = relay.at[relay_at[hops[2]], half]
        wire.arrived(relayed[hops[2]], last, to(hops[2]))
        cut = V // 2
        top, bottom = total[:cut], total[cut:]
        if o == 3:
            top = top + last[...].astype(F32)
        else:
            bottom = bottom + last[...].astype(F32)
        ready[o, low] = top.astype(BF16)
        ready[o, high] = bottom.astype(BF16)
        wire.start(direct[o], ready.at[o], final.at[relay_at[o]], to(o))
    yield
    total = value(0)
    for o in (1, 11, 2, 10, 3, 9):
        wire.arrived(direct[o], final.at[relay_at[o]], to(o))
        total = total + final[relay_at[o]].astype(F32)
    done(total)


def col_reduce(wire, me, partial, core_buf, cross_out, cross_buf, ready, final, done):
    sibling, partner = me.at(core=1 - me.core), me.at(x_hi=1 - me.x_hi)
    order = (4, 5, 3, 7, 1, 6, 2, 0)
    early = (4, 5, 3, 6, 2)
    cores = {o: wire.slot() for o in order}
    cross = {o: wire.slot() for o in early + (0,)}
    direct = {o: wire.slot() for o in order[:-1]}
    side = {o: wire.slot() for o in (1, 7)}
    side_at = {1: Y, 7: Y + 1}
    spot = lambda o: (me.y + o) % Y
    to = lambda o: me.at(y=spot(o))

    def pair_sum(o, x_hi):
        return partial[me.core, spot(o), x_hi].astype(F32) + core_buf[spot(o), x_hi].astype(F32)

    for o in order:
        wire.start(cores[o], partial.at[1 - me.core, spot(o)], core_buf.at[spot(o)], sibling)
    for o in order:
        wire.arrived(cores[o], core_buf.at[spot(o)], sibling)
        if o:
            cross_out[o] = pair_sum(o, 1 - me.x_hi).astype(BF16)
        if o in early:
            wire.start(cross[o], cross_out.at[o], cross_buf.at[spot(o)], partner)
        elif o:
            wire.start(side[o], cross_out.at[o], final.at[side_at[o]], to(o))
            ready[o] = pair_sum(o, me.x_hi).astype(BF16)
            wire.start(direct[o], ready.at[o], final.at[o], to(o))

    def value(o):
        wire.arrived(cross[o], cross_buf.at[spot(o)], partner)
        return pair_sum(o, me.x_hi) + cross_buf[spot(o)].astype(F32)

    for o in early:
        ready[o] = value(o).astype(BF16)
        wire.start(direct[o], ready.at[o], final.at[o], to(o))
        if o == 3:
            total = pair_sum(0, 1 - me.x_hi)
            for near in (1, 7):
                wire.arrived(side[near], final.at[side_at[near]], to(near))
                total = total + final[side_at[near]].astype(F32)
            cross_out[0] = total.astype(BF16)
            wire.start(cross[0], cross_out.at[0], cross_buf.at[me.y], partner)
    total = value(0)
    for o in (7, 1, 4, 5, 3, 6, 2):
        wire.arrived(direct[o], final.at[o], to(o))
        total = total + final[o].astype(F32)
    done(total)


def col_gather(wire, me, row_block):
    sibling, partner = me.at(core=1 - me.core), me.at(x_hi=1 - me.x_hi)

    def block(offset, x_hi, core=me.core):
        return row_block.at[core, (me.y + offset) % Y, x_hi]

    direct = {o: wire.slot() for o in range(1, Y)}
    cross = {o: wire.slot() for o in (0, 5, 3, 6, 2, 4)}
    side = {o: wire.slot() for o in (1, 7)}
    mine = {o: wire.slot() for o in range(Y)}
    theirs = {o: wire.slot() for o in range(Y)}
    own, other = block(0, me.x_hi), 1 - me.x_hi
    to = lambda o: me.at(y=(me.y + o) % Y)

    def hand_over(o):
        here = block(o, me.x_hi)
        if o in cross:
            wire.start(cross[o], here, here, partner)
        wire.start(mine[o], here, here, sibling)

    def pass_on(slot, o, sender):
        here = block(o, other)
        wire.arrived(slot, here, sender)
        wire.start(theirs[o], here, here, sibling)

    for o in (4, 3, 5, 2, 6, 1, 7):
        wire.start(direct[o], own, own, to(o))
    hand_over(0)
    yield
    wire.arrived(cross[0], block(0, other), partner)
    for o in side:
        wire.start(side[o], block(0, other), block(0, other), to(o))
    wire.start(theirs[0], block(0, other), block(0, other), sibling)
    for o in (3, 5, 2, 6):
        wire.arrived(direct[o], block(Y - o, me.x_hi), to(o))
        hand_over(Y - o)
    yield
    for o in (4, 1, 7):
        wire.arrived(direct[o], block(Y - o, me.x_hi), to(o))
        hand_over(Y - o)
    yield
    for o in (5, 3):
        pass_on(cross[o], o, partner)
    for o in side:
        pass_on(side[o], Y - o, to(o))
    yield
    for o in (6, 2, 4):
        pass_on(cross[o], o, partner)
    yield
    for o in range(Y):
        wire.arrived(mine[o], block(o, me.x_hi, 1 - me.core), sibling)
        wire.arrived(theirs[o], block(o, other, 1 - me.core), sibling)


def together(*jobs):
    jobs = list(jobs)
    while jobs:
        for job in list(jobs):
            try:
                next(job)
            except StopIteration:
                jobs.remove(job)


def in_turn(first, second, order):
    for letter in order:
        next(first if letter == "A" else second, None)
    together(first, second)


def column_of(row_vector):
    return jnp.transpose(jnp.broadcast_to(row_vector, (V, V)))


def unpack(words):
    parts = []
    for half in (0, 1):
        part = words[16 * half:16 * half + 16]
        for k in range(8):
            parts.append(jnp.bitwise_and(jnp.right_shift(part, k), 1).astype(F32).astype(BF16))
    return jnp.concatenate(parts, axis=0)


def gather_kernel(count, features, scale, bits, out, masks, send, recv):
    me = Place()
    peers = [me.at(z=(me.z + d) % Z) for d in (1, 2, 3, 9, 10, 11)]
    ready = greet(peers + [me.at(x_lo=1 - me.x_lo)])
    scaled = features[...].astype(F32) * column_of(scale[...].astype(F32))
    out[me.row] = scaled.astype(BF16)
    ready()
    wire = Wire(send, recv)
    gathering = row_gather(wire, me, out)
    next(gathering)
    live = count[0]

    def turn(t, _):
        masks[t] = unpack(jnp.where(t < live, bits[t], 0))
        return 0

    lax.fori_loop(0, bits.shape[0], turn, 0)
    together(gathering)
    wire.finish()


UNROLL = 4


def live_tiles(count, body):
    def turn(step, _):
        for u in range(UNROLL):
            body(step * UNROLL + u)
        return 0

    lax.fori_loop(0, (count[0] + UNROLL - 1) // UNROLL, turn, 0)


def forward_kernel(rows, cols, count, source, masks, out, acc):
    acc[...] = jnp.zeros_like(acc)

    def body(slot):
        i = rows[slot]
        acc[i] = acc[i] + jnp.dot(masks[slot], source[cols[slot]], preferred_element_type=F32)

    live_tiles(count, body)
    for i in range(acc.shape[0]):
        for half in (0, 1):
            out[half, i % Y, i // Y] = acc[i, half * V:half * V + V, :].astype(BF16)


def backward_kernel(rows, cols, count, source, masks, act_in, out, act_out, acc):
    acc[...] = jnp.zeros_like(acc)
    act_out[...] = act_in[...]

    def body(slot):
        i, j = rows[slot], cols[slot]
        y, x_hi = i % Y, i // Y
        back = jnp.concatenate([source[0, y, x_hi], source[1, y, x_hi]], axis=1)
        acc[j] = acc[j] + jnp.dot(back, masks[slot], preferred_element_type=F32)

    live_tiles(count, body)
    for j in range(acc.shape[0]):
        for half in (0, 1):
            out[2 * j + half] = acc[j, :, half * V:half * V + V].astype(BF16)


def vertex_kernel(partial, scale, weight, cotangent, act, row_block, piece,
                  core_buf, cross_out, cross_buf, outgoing, final, natural, grad, grad_core, grad_mine,
                  grad_y, grad_x, send, recv):
    me = Place()
    partner, sibling = me.at(x_hi=1 - me.x_hi), me.at(core=1 - me.core)
    y_peers = [me.at(y=(me.y + d) % Y) for d in range(1, Y)]
    x_ring = {(lo, hi): me.at(x_lo=(me.x_lo + lo) % X_LO, x_hi=(me.x_hi + hi) % X_HI)
              for lo, hi in ((0, 1), (1, 0), (1, 1))}
    ready = greet([sibling] + y_peers + list(x_ring.values()))
    wire = Wire(send, recv)
    scale_row = scale[...].astype(F32)
    scale_col = column_of(scale_row)
    ready()
    pieces = []
    col_reduce(wire, me, partial, core_buf, cross_out, cross_buf, outgoing, final, pieces.append)
    summed = pieces[0]
    for k in range(8):
        natural[pl.ds(k, 16, stride=8), :] = summed[16 * k:16 * k + 16]
    hidden = (natural[...] * scale_col).astype(BF16)
    pre_act = jnp.dot(hidden, weight[...], preferred_element_type=F32)
    sigmoid = 1.0 / (1.0 + jnp.exp(-pre_act))
    slope = sigmoid * (1.0 + pre_act * (1.0 - sigmoid))
    slope_term = (cotangent[...].astype(F32) * slope).astype(BF16)
    back = lax.dot_general(weight[...], slope_term, (((1,), (1,)), ((), ())),
                           preferred_element_type=F32)
    back = (back * scale_row).astype(BF16)
    from_v = lax.broadcasted_iota(jnp.int32, (V, V), 0)
    to_v = lax.broadcasted_iota(jnp.int32, (V, V), 1)
    swap = (from_v == 8 * (to_v % 16) + to_v // 16).astype(F32).astype(BF16)
    row_block[me.core, me.y, me.x_hi] = jnp.dot(
        back, swap, preferred_element_type=F32).astype(BF16)

    def weight_part():
        act[...] = (pre_act * sigmoid).astype(BF16)
        grad[...] = lax.dot_general(hidden, slope_term, (((0,), (0,)), ((), ())),
                                    preferred_element_type=F32).reshape(2, V // 2, 2 * V)
        slot = wire.slot()
        wire.start(slot, grad.at[1 - me.core], grad_core, sibling)
        yield
        wire.arrived(slot, grad_core, sibling)
        grad_mine[...] = (grad[me.core] + grad_core[...]).reshape(Y, V // 16, 2 * V)
        slots = [wire.slot() for _ in y_peers]
        for d, peer in enumerate(y_peers, 1):
            wire.start(slots[d - 1], grad_mine.at[(me.y + d) % Y], grad_y.at[me.y], peer)
        grad_y[me.y] = grad_mine[me.y]
        yield
        for d, peer in enumerate(y_peers, 1):
            wire.arrived(slots[d - 1], grad_y.at[(me.y + Y - d) % Y], peer)
        total = grad_y[0]
        for k in range(1, Y):
            total = total + grad_y[k]
        place = lambda lo, hi: grad_x.at[((me.x_lo + lo) % X_LO) * X_HI + (me.x_hi + hi) % X_HI]
        place(0, 0)[...] = total
        slots = {shift: wire.slot() for shift in x_ring}
        for shift in x_ring:
            wire.start(slots[shift], place(0, 0), place(0, 0), x_ring[shift])
        yield
        for shift in x_ring:
            wire.arrived(slots[shift], place(*shift), x_ring[shift])
        total = grad_x[0]
        for k in range(1, X_LO * X_HI):
            total = total + grad_x[k]
        piece[...] = total

    in_turn(col_gather(wire, me, row_block), weight_part(), "ABBABAB")
    wire.finish()


def scatter_kernel(partial, scale, piece, grad_in, weight_grad, cross_buf, outgoing, relay, final,
                   sums, send, recv):
    me = Place()
    partner, sibling = me.at(x_lo=1 - me.x_lo), me.at(core=1 - me.core)
    z_near = {o: me.at(z=(me.z + o) % Z) for o in (1, 2, 3, 9, 10, 11)}
    y_peers = [me.at(y=(me.y + d) % Y) for d in range(1, Y)]
    ready = greet([partner, sibling] + y_peers + list(z_near.values()))
    wire = Wire(send, recv)
    scale_row = scale[...].astype(F32)
    ready()

    def done(total):
        grad_in[...] = jnp.transpose(total * scale_row).astype(BF16)

    def weight_part():
        at = lambda offset: sums.at[(me.z + offset) % Z]
        near = {o: wire.slot() for o in (3, 9, 2, 10, 1, 11)}
        far = {o: wire.slot() for o in (3, 2, 10, 1, 11)}
        at(0)[...] = piece[...]
        for o in near:
            wire.start(near[o], at(0), at(0), z_near[o])
        yield
        for o in near:
            wire.arrived(near[o], at(Z - o), z_near[o])
            if o in (3, 9):
                for hop in ((3, 2, 1) if o == 3 else (10, 11)):
                    wire.start(far[hop], at(Z - o), at(Z - o), z_near[hop])
        yield
        for o, source in ((1, 8), (11, 4), (2, 7), (10, 5), (3, 6)):
            wire.arrived(far[o], at(source), z_near[o])
        total = sums[0]
        for k in range(1, Z):
            total = total + sums[k]
        spot = weight_grad.at[me.core, me.y]
        spot[...] = total / math.sqrt(X_LO * Z * X_HI * Y * CORES * V)
        slots = [wire.slot() for _ in y_peers]
        for d, peer in enumerate(y_peers, 1):
            wire.start(slots[d - 1], spot, spot, peer)
        yield
        for d, peer in enumerate(y_peers, 1):
            wire.arrived(slots[d - 1], weight_grad.at[me.core, (me.y + Y - d) % Y], peer)
        slot = wire.slot()
        wire.start(slot, weight_grad.at[me.core], weight_grad.at[me.core], sibling)
        yield
        wire.arrived(slot, weight_grad.at[1 - me.core], sibling)

    in_turn(row_reduce(wire, me, partial, cross_buf, outgoing, relay, final, done), weight_part(),
            "ABABABABA")
    wire.finish()


def sems(count):
    return [pltpu.SemaphoreType.DMA((count,)), pltpu.SemaphoreType.DMA((count,))]


def shape(extent, dtype):
    return jax.ShapeDtypeStruct(extent, dtype)


def talking(collective_id):
    return pltpu.CompilerParams(
        collective_id=collective_id, has_side_effects=True, vmem_limit_bytes=VMEM_BYTES)


def gather_call(count, features, scale, bits):
    return pl.pallas_call(
        gather_kernel,
        out_shape=(shape((X_LO * Z, V, V), BF16), shape((bits.shape[0], 2 * V, 2 * V), BF16)),
        in_specs=[SCALARS] + [WHOLE] * 3,
        out_specs=(WHOLE,) * 2,
        scratch_shapes=sems(24),
        compiler_params=talking(0),
        name="gather_rows",
    )(count, features, scale, bits)


def forward_call(rows, cols, count, source, masks):
    return pl.pallas_call(
        forward_kernel,
        out_shape=shape((CORES, Y, X_HI, V, V), BF16),
        in_specs=[SCALARS] * 3 + [WHOLE] * 2,
        out_specs=WHOLE,
        scratch_shapes=[pltpu.VMEM((X_HI * Y, 2 * V, V), F32)],
        compiler_params=pltpu.CompilerParams(vmem_limit_bytes=VMEM_BYTES),
        name="forward_tiles",
    )(rows, cols, count, source, masks)


def vertex_call(partial, scale, weight, cotangent):
    return pl.pallas_call(
        vertex_kernel,
        out_shape=(shape((V, 2 * V), BF16), shape((CORES, Y, X_HI, V, V), BF16), shape((8, 2 * V), F32)),
        in_specs=[WHOLE] * 4,
        out_specs=(WHOLE,) * 3,
        scratch_shapes=[
            pltpu.VMEM((Y, X_HI, V, V), BF16),
            pltpu.VMEM((Y, V, V), BF16),
            pltpu.VMEM((Y, V, V), BF16),
            pltpu.VMEM((Y, V, V), BF16),
            pltpu.VMEM((Y + 2, V, V), BF16),
            pltpu.VMEM((V, V), F32),
            pltpu.VMEM((2, V // 2, 2 * V), F32),
            pltpu.VMEM((V // 2, 2 * V), F32),
            pltpu.VMEM((Y, 8, 2 * V), F32),
            pltpu.VMEM((Y, 8, 2 * V), F32),
            pltpu.VMEM((X_LO * X_HI, 8, 2 * V), F32),
        ] + sems(72),
        compiler_params=talking(1),
        name="vertex_part",
    )(partial, scale, weight, cotangent)


def backward_call(rows, cols, count, source, masks, act):
    return pl.pallas_call(
        backward_kernel,
        out_shape=(shape((X_LO * Z, V, V), BF16), shape(act.shape, act.dtype)),
        in_specs=[SCALARS] * 3 + [WHOLE] * 3,
        out_specs=(WHOLE,) * 2,
        scratch_shapes=[pltpu.VMEM((X_LO * Z // 2, V, 2 * V), F32)],
        compiler_params=pltpu.CompilerParams(vmem_limit_bytes=VMEM_BYTES),
        name="backward_tiles",
    )(rows, cols, count, source, masks, act)


def scatter_call(partial, scale, piece):
    return pl.pallas_call(
        scatter_kernel,
        out_shape=(shape((V, V), BF16), shape((CORES, Y, 8, 2 * V), F32)),
        in_specs=[WHOLE] * 3,
        out_specs=(WHOLE,) * 2,
        scratch_shapes=[
            pltpu.VMEM((Z, V, V), BF16),
            pltpu.VMEM((Z, V, V), BF16),
            pltpu.VMEM((8, V, V), BF16),
            pltpu.VMEM((6, V, V), BF16),
            pltpu.VMEM((Z, 8, 2 * V), F32),
        ] + sems(48),
        compiler_params=talking(2),
        name="scatter_rows",
    )(partial, scale, piece)


def on_device(features, deg_scale, weight, cotangent, tile_rows, tile_cols, tile_count, tile_bits):
    rows, cols, count, bits = tile_rows[0, 0], tile_cols[0, 0], tile_count[0], tile_bits[0, 0]
    scale = deg_scale.reshape(1, V)
    column_block, masks = gather_call(count, features, scale, bits)
    partial = forward_call(rows, cols, count, column_block.reshape(Z, 2 * V, V), masks)
    act, row_block, piece = vertex_call(partial, scale, weight, cotangent)
    partial_back, activations = backward_call(rows, cols, count, row_block, masks, act)
    input_grad, grad = scatter_call(partial_back, scale, piece)
    weight_grad = grad.reshape(V, 2 * V)
    return (activations, input_grad, weight_grad)


def solution(mesh):
    in_specs = (
        P(("row", "col"), None),
        P(("row", "col")),
        P(),
        P(("row", "col"), None),
        P("row", "col", None),
        P("row", "col", None),
        P("row", "col"),
        P("row", "col", None, None, None),
    )
    out_specs = (P(("row", "col"), None), P(("row", "col"), None), P())
    return jax.shard_map(
        on_device, mesh=mesh, in_specs=in_specs, out_specs=out_specs, check_vma=False)
```

```python
import functools
import math

import jax
import jax.numpy as jnp
from jax import lax
from jax.experimental import pallas as pl
from jax.experimental.pallas import tpu as pltpu
from jax.sharding import PartitionSpec as P

MESH = pl.DeviceIdType.MESH
F32, BF16 = jnp.float32, jnp.bfloat16
X_LO, Z = 2, 12
X_HI, Y, CORES = 2, 8, 2
V = 128
VMEM_BYTES = 24 * 1024 * 1024
WHOLE = pl.BlockSpec(memory_space=pltpu.VMEM)
SCALARS = pl.BlockSpec(memory_space=pltpu.SMEM)


class Place:
    def __init__(self):
        row, col = lax.axis_index("row"), lax.axis_index("col")
        self.row, self.col = row, col
        self.x_lo, self.z = row // Z, row % Z
        self.x_hi, self.y, self.core = col // (Y * CORES), (col // CORES) % Y, col % CORES

    def at(self, x_lo=None, z=None, x_hi=None, y=None, core=None):
        x_lo = self.x_lo if x_lo is None else x_lo
        z = self.z if z is None else z
        x_hi = self.x_hi if x_hi is None else x_hi
        y = self.y if y is None else y
        core = self.core if core is None else core
        return (x_lo * Z + z, (x_hi * Y + y) * CORES + core)


def greet(peers):
    barrier = pltpu.get_barrier_semaphore()
    for peer in peers:
        pl.semaphore_signal(barrier, inc=1, device_id=peer, device_id_type=MESH)
    return lambda: pl.semaphore_wait(barrier, len(peers))


class Wire:
    def __init__(self, send, recv):
        self.send, self.recv, self.used, self.sent = send, recv, 0, []

    def slot(self):
        self.used += 1
        return self.used - 1

    def copy(self, slot, src, dst, to):
        return pltpu.make_async_remote_copy(
            src_ref=src, dst_ref=dst, send_sem=self.send.at[slot], recv_sem=self.recv.at[slot],
            device_id=to, device_id_type=MESH)

    def start(self, slot, src, dst, to):
        copy = self.copy(slot, src, dst, to)
        copy.start()
        self.sent.append(copy)

    def arrived(self, slot, dst, to):
        self.copy(slot, dst, dst, to).wait_recv()

    def finish(self):
        for copy in self.sent:
            copy.wait_send()


def row_gather(wire, me, out):
    def block(offset, pair=me.x_lo):
        return out.at[pair * Z + (me.z + offset) % Z]

    def to(offset):
        return me.at(z=(me.z + offset) % Z)

    partner, other = me.at(x_lo=1 - me.x_lo), 1 - me.x_lo
    near = {o: wire.slot() for o in (3, 9, 2, 10, 1, 11)}
    far = {o: wire.slot() for o in (3, 9, 2, 10, 1, 11)}
    cross = {o: wire.slot() for o in (0, 9, 3, 10, 2, 7, 5, 6)}
    side = {o: wire.slot() for o in (1, 11)}
    side_far = {o: wire.slot() for o in (1, 11)}

    def hand_over(offset):
        wire.start(cross[offset], block(offset), block(offset), partner)

    for o in near:
        wire.start(near[o], block(0), block(0), to(o))
    hand_over(0)
    yield
    wire.arrived(cross[0], block(0, other), partner)
    for o in side:
        wire.start(side[o], block(0, other), block(0, other), to(o))
    for o in near:
        source = Z - o
        wire.arrived(near[o], block(source), to(o))
        if o in (3, 9):
            sign = 1 if o == 3 else -1
            half = block(source).at[pl.ds(0 if o == 3 else V // 2, V // 2)]
            wire.start(far[o], half, half, to(3 * sign % Z))
            wire.start(far[2 * sign % Z], block(source), block(source), to(2 * sign % Z))
            wire.start(far[sign % Z], block(source), block(source), to(sign % Z))
        if o not in side:
            hand_over(source)
    yield
    for o, source in ((1, 9), (11, 3)):
        wire.arrived(cross[source], block(source, other), partner)
        wire.start(side_far[o], block(source, other), block(source, other), to(o))
    for o, source in ((2, 7), (10, 5)):
        wire.arrived(far[o], block(source), to(o))
        hand_over(source)
    wire.arrived(far[3], block(6).at[pl.ds(0, V // 2)], to(3))
    wire.arrived(far[9], block(6).at[pl.ds(V // 2, V // 2)], to(9))
    hand_over(6)
    yield
    for o, source in ((1, 8), (11, 4)):
        wire.arrived(far[o], block(source), to(o))
        wire.arrived(side[o], block(Z - o, other), to(o))
        wire.arrived(side_far[o], block(source, other), to(o))
    for o in (10, 2, 7, 5, 6):
        wire.arrived(cross[o], block(o, other), partner)


def row_reduce(wire, me, partial, cross_buf, ready, relay, final, done):
    def to(offset):
        return me.at(z=(me.z + offset) % Z)

    def term(pair, offset):
        return partial.at[pair * Z + (me.z + offset) % Z]

    partner, other = me.at(x_lo=1 - me.x_lo), 1 - me.x_lo
    order = (4, 8, 5, 7, 6, 3, 9, 2, 10)
    cross = {o: wire.slot() for o in order + (0,)}
    direct = {o: wire.slot() for o in (2, 10, 1, 11, 3, 9)}
    side = {o: wire.slot() for o in (1, 11)}
    relay_at = {1: 0, 11: 1, 2: 2, 10: 3, 3: 4, 9: 5}
    side_at = {1: 6, 11: 7}
    for o in order:
        wire.start(cross[o], term(other, o), cross_buf.at[(me.z + o) % Z], partner)
    for o in (1, 11):
        wire.start(side[o], term(other, o), relay.at[side_at[o]], to(o))
        wire.start(direct[o], term(me.x_lo, o), final.at[relay_at[o]], to(o))

    def value(offset):
        t = (me.z + offset) % Z
        wire.arrived(cross[offset], cross_buf.at[t], partner)
        return term(me.x_lo, offset)[...].astype(F32) + cross_buf[t].astype(F32)

    yield
    relayed = {o: wire.slot() for o in (1, 11, 2, 10, 3, 9)}
    low, high = pl.ds(0, V // 2), pl.ds(V // 2, V // 2)
    for some in (((4, 1), (8, 11)), ((5, 2), (7, 10))):
        for o, hop in some:
            ready[o] = value(o).astype(BF16)
            wire.start(relayed[hop], ready.at[o], relay.at[relay_at[hop]], to(hop))
        if o == 8:
            yield
    ready[6] = value(6).astype(BF16)
    for hop, half in ((3, low), (9, high)):
        wire.start(relayed[hop], ready.at[6, half], relay.at[relay_at[hop], half], to(hop))
    total = term(other, 0)[...].astype(F32)
    for o in (1, 11):
        wire.arrived(side[o], relay.at[side_at[o]], to(o))
        total = total + relay[side_at[o]].astype(F32)
    ready[0] = total.astype(BF16)
    wire.start(cross[0], ready.at[0], cross_buf.at[me.z], partner)
    yield
    sums = {o: value(o) for o in (3, 9)}
    for o in (2, 10):
        ready[o] = value(o).astype(BF16)
        wire.start(direct[o], ready.at[o], final.at[relay_at[o]], to(o))
    yield
    for o, hops, half in ((3, (1, 2, 3), low), (9, (11, 10, 9), high)):
        total = sums[o]
        for hop in hops[:2]:
            wire.arrived(relayed[hop], relay.at[relay_at[hop]], to(hop))
            total = total + relay[relay_at[hop]].astype(F32)
        last = relay.at[relay_at[hops[2]], half]
        wire.arrived(relayed[hops[2]], last, to(hops[2]))
        cut = V // 2
        top, bottom = total[:cut], total[cut:]
        if o == 3:
            top = top + last[...].astype(F32)
        else:
            bottom = bottom + last[...].astype(F32)
        ready[o, low] = top.astype(BF16)
        ready[o, high] = bottom.astype(BF16)
        wire.start(direct[o], ready.at[o], final.at[relay_at[o]], to(o))
    yield
    total = value(0)
    for o in (1, 11, 2, 10, 3, 9):
        wire.arrived(direct[o], final.at[relay_at[o]], to(o))
        total = total + final[relay_at[o]].astype(F32)
    done(total)


def col_reduce(wire, me, partial, core_buf, cross_out, cross_buf, ready, final, done):
    sibling, partner = me.at(core=1 - me.core), me.at(x_hi=1 - me.x_hi)
    order = (4, 5, 3, 7, 1, 6, 2, 0)
    early = (4, 5, 3, 6, 2)
    cores = {o: wire.slot() for o in order}
    cross = {o: wire.slot() for o in early + (0,)}
    direct = {o: wire.slot() for o in order[:-1]}
    side = {o: wire.slot() for o in (1, 7)}
    side_at = {1: Y, 7: Y + 1}
    spot = lambda o: (me.y + o) % Y
    to = lambda o: me.at(y=spot(o))

    def pair_sum(o, x_hi):
        return partial[me.core, spot(o), x_hi].astype(F32) + core_buf[spot(o), x_hi].astype(F32)

    for o in order:
        wire.start(cores[o], partial.at[1 - me.core, spot(o)], core_buf.at[spot(o)], sibling)
    for o in order:
        wire.arrived(cores[o], core_buf.at[spot(o)], sibling)
        if o:
            cross_out[o] = pair_sum(o, 1 - me.x_hi).astype(BF16)
        if o in early:
            wire.start(cross[o], cross_out.at[o], cross_buf.at[spot(o)], partner)
        elif o:
            wire.start(side[o], cross_out.at[o], final.at[side_at[o]], to(o))
            ready[o] = pair_sum(o, me.x_hi).astype(BF16)
            wire.start(direct[o], ready.at[o], final.at[o], to(o))

    def value(o):
        wire.arrived(cross[o], cross_buf.at[spot(o)], partner)
        return pair_sum(o, me.x_hi) + cross_buf[spot(o)].astype(F32)

    for o in early:
        ready[o] = value(o).astype(BF16)
        wire.start(direct[o], ready.at[o], final.at[o], to(o))
        if o == 3:
            total = pair_sum(0, 1 - me.x_hi)
            for near in (1, 7):
                wire.arrived(side[near], final.at[side_at[near]], to(near))
                total = total + final[side_at[near]].astype(F32)
            cross_out[0] = total.astype(BF16)
            wire.start(cross[0], cross_out.at[0], cross_buf.at[me.y], partner)
    total = value(0)
    for o in (7, 1, 4, 5, 3, 6, 2):
        wire.arrived(direct[o], final.at[o], to(o))
        total = total + final[o].astype(F32)
    done(total)


def col_gather(wire, me, row_block):
    sibling, partner = me.at(core=1 - me.core), me.at(x_hi=1 - me.x_hi)

    def block(offset, x_hi, core=me.core):
        return row_block.at[core, (me.y + offset) % Y, x_hi]

    direct = {o: wire.slot() for o in range(1, Y)}
    cross = {o: wire.slot() for o in (0, 5, 3, 6, 2, 4)}
    side = {o: wire.slot() for o in (1, 7)}
    mine = {o: wire.slot() for o in range(Y)}
    theirs = {o: wire.slot() for o in range(Y)}
    own, other = block(0, me.x_hi), 1 - me.x_hi
    to = lambda o: me.at(y=(me.y + o) % Y)

    def hand_over(o):
        here = block(o, me.x_hi)
        if o in cross:
            wire.start(cross[o], here, here, partner)
        wire.start(mine[o], here, here, sibling)

    def pass_on(slot, o, sender):
        here = block(o, other)
        wire.arrived(slot, here, sender)
        wire.start(theirs[o], here, here, sibling)

    for o in (4, 3, 5, 2, 6, 1, 7):
        wire.start(direct[o], own, own, to(o))
    hand_over(0)
    yield
    wire.arrived(cross[0], block(0, other), partner)
    for o in side:
        wire.start(side[o], block(0, other), block(0, other), to(o))
    wire.start(theirs[0], block(0, other), block(0, other), sibling)
    for o in (3, 5, 2, 6):
        wire.arrived(direct[o], block(Y - o, me.x_hi), to(o))
        hand_over(Y - o)
    yield
    for o in (4, 1, 7):
        wire.arrived(direct[o], block(Y - o, me.x_hi), to(o))
        hand_over(Y - o)
    yield
    for o in (5, 3):
        pass_on(cross[o], o, partner)
    for o in side:
        pass_on(side[o], Y - o, to(o))
    yield
    for o in (6, 2, 4):
        pass_on(cross[o], o, partner)
    yield
    for o in range(Y):
        wire.arrived(mine[o], block(o, me.x_hi, 1 - me.core), sibling)
        wire.arrived(theirs[o], block(o, other, 1 - me.core), sibling)


def together(*jobs):
    jobs = list(jobs)
    while jobs:
        for job in list(jobs):
            try:
                next(job)
            except StopIteration:
                jobs.remove(job)


def in_turn(first, second, order):
    for letter in order:
        next(first if letter == "A" else second, None)
    together(first, second)


def column_of(row_vector):
    return jnp.transpose(jnp.broadcast_to(row_vector, (V, V)))


def unpack(words):
    parts = []
    for half in (0, 1):
        part = words[16 * half:16 * half + 16]
        for k in range(8):
            parts.append(jnp.bitwise_and(jnp.right_shift(part, k), 1).astype(F32).astype(BF16))
    return jnp.concatenate(parts, axis=0)


def gather_kernel(count, features, scale, bits, out, masks, send, recv):
    me = Place()
    peers = [me.at(z=(me.z + d) % Z) for d in (1, 2, 3, 9, 10, 11)]
    ready = greet(peers + [me.at(x_lo=1 - me.x_lo)])
    scaled = features[...].astype(F32) * column_of(scale[...].astype(F32))
    out[me.row] = scaled.astype(BF16)
    ready()
    wire = Wire(send, recv)
    gathering = row_gather(wire, me, out)
    next(gathering)
    live = count[0]

    def turn(t, _):
        masks[t] = unpack(jnp.where(t < live, bits[t], 0))
        return 0

    lax.fori_loop(0, bits.shape[0], turn, 0)
    together(gathering)
    wire.finish()


UNROLL = 4


def live_tiles(count, product, place, acc):
    def turn(step, _):
        slots = [step * UNROLL + u for u in range(UNROLL)]
        products = [product(slot) for slot in slots]
        for slot, value in zip(slots, products):
            acc[place(slot)] = acc[place(slot)] + value
        return 0

    lax.fori_loop(0, (count[0] + UNROLL - 1) // UNROLL, turn, 0)


def forward_kernel(rows, cols, count, source, masks, out, acc):
    acc[...] = jnp.zeros_like(acc)

    def product(slot):
        return jnp.dot(masks[slot], source[cols[slot]], preferred_element_type=F32)

    live_tiles(count, product, lambda slot: rows[slot], acc)
    for i in range(acc.shape[0]):
        for half in (0, 1):
            out[half, i % Y, i // Y] = acc[i, half * V:half * V + V, :].astype(BF16)


def backward_kernel(rows, cols, count, source, masks, act_in, out, act_out, acc):
    acc[...] = jnp.zeros_like(acc)
    act_out[...] = act_in[...]

    def product(slot):
        i = rows[slot]
        y, x_hi = i % Y, i // Y
        back = jnp.concatenate([source[0, y, x_hi], source[1, y, x_hi]], axis=1)
        return jnp.dot(back, masks[slot], preferred_element_type=F32)

    live_tiles(count, product, lambda slot: cols[slot], acc)
    for j in range(acc.shape[0]):
        for half in (0, 1):
            out[2 * j + half] = acc[j, :, half * V:half * V + V].astype(BF16)


def vertex_kernel(partial, scale, weight, cotangent, act, row_block, piece,
                  core_buf, cross_out, cross_buf, outgoing, final, natural, grad, grad_core, grad_mine,
                  grad_y, grad_x, send, recv):
    me = Place()
    partner, sibling = me.at(x_hi=1 - me.x_hi), me.at(core=1 - me.core)
    y_peers = [me.at(y=(me.y + d) % Y) for d in range(1, Y)]
    x_ring = {(lo, hi): me.at(x_lo=(me.x_lo + lo) % X_LO, x_hi=(me.x_hi + hi) % X_HI)
              for lo, hi in ((0, 1), (1, 0), (1, 1))}
    ready = greet([sibling] + y_peers + list(x_ring.values()))
    wire = Wire(send, recv)
    scale_row = scale[...].astype(F32)
    scale_col = column_of(scale_row)
    ready()
    pieces = []
    col_reduce(wire, me, partial, core_buf, cross_out, cross_buf, outgoing, final, pieces.append)
    summed = pieces[0]
    for k in range(8):
        natural[pl.ds(k, 16, stride=8), :] = summed[16 * k:16 * k + 16]
    hidden = (natural[...] * scale_col).astype(BF16)
    pre_act = jnp.dot(hidden, weight[...], preferred_element_type=F32)
    sigmoid = 1.0 / (1.0 + jnp.exp(-pre_act))
    slope = sigmoid * (1.0 + pre_act * (1.0 - sigmoid))
    slope_term = (cotangent[...].astype(F32) * slope).astype(BF16)
    back = lax.dot_general(weight[...], slope_term, (((1,), (1,)), ((), ())),
                           preferred_element_type=F32)
    back = (back * scale_row).astype(BF16)
    from_v = lax.broadcasted_iota(jnp.int32, (V, V), 0)
    to_v = lax.broadcasted_iota(jnp.int32, (V, V), 1)
    swap = (from_v == 8 * (to_v % 16) + to_v // 16).astype(F32).astype(BF16)
    row_block[me.core, me.y, me.x_hi] = jnp.dot(
        back, swap, preferred_element_type=F32).astype(BF16)

    def weight_part():
        act[...] = (pre_act * sigmoid).astype(BF16)
        grad[...] = lax.dot_general(hidden, slope_term, (((0,), (0,)), ((), ())),
                                    preferred_element_type=F32).reshape(2, V // 2, 2 * V)
        slot = wire.slot()
        wire.start(slot, grad.at[1 - me.core], grad_core, sibling)
        yield
        wire.arrived(slot, grad_core, sibling)
        grad_mine[...] = (grad[me.core] + grad_core[...]).reshape(Y, V // 16, 2 * V)
        slots = [wire.slot() for _ in y_peers]
        for d, peer in enumerate(y_peers, 1):
            wire.start(slots[d - 1], grad_mine.at[(me.y + d) % Y], grad_y.at[me.y], peer)
        grad_y[me.y] = grad_mine[me.y]
        yield
        for d, peer in enumerate(y_peers, 1):
            wire.arrived(slots[d - 1], grad_y.at[(me.y + Y - d) % Y], peer)
        total = grad_y[0]
        for k in range(1, Y):
            total = total + grad_y[k]
        place = lambda lo, hi: grad_x.at[((me.x_lo + lo) % X_LO) * X_HI + (me.x_hi + hi) % X_HI]
        place(0, 0)[...] = total
        slots = {shift: wire.slot() for shift in x_ring}
        for shift in x_ring:
            wire.start(slots[shift], place(0, 0), place(0, 0), x_ring[shift])
        yield
        for shift in x_ring:
            wire.arrived(slots[shift], place(*shift), x_ring[shift])
        total = grad_x[0]
        for k in range(1, X_LO * X_HI):
            total = total + grad_x[k]
        piece[...] = total

    in_turn(col_gather(wire, me, row_block), weight_part(), "ABBABAAB")
    wire.finish()


def scatter_kernel(partial, scale, piece, grad_in, weight_grad, cross_buf, outgoing, relay, final,
                   sums, send, recv):
    me = Place()
    partner, sibling = me.at(x_lo=1 - me.x_lo), me.at(core=1 - me.core)
    z_near = {o: me.at(z=(me.z + o) % Z) for o in (1, 2, 3, 9, 10, 11)}
    y_peers = [me.at(y=(me.y + d) % Y) for d in range(1, Y)]
    ready = greet([partner, sibling] + y_peers + list(z_near.values()))
    wire = Wire(send, recv)
    scale_row = scale[...].astype(F32)
    ready()

    def done(total):
        grad_in[...] = jnp.transpose(total * scale_row).astype(BF16)

    def weight_part():
        at = lambda offset: sums.at[(me.z + offset) % Z]
        near = {o: wire.slot() for o in (3, 9, 2, 10, 1, 11)}
        far = {o: wire.slot() for o in (3, 2, 10, 1, 11)}
        at(0)[...] = piece[...]
        for o in near:
            wire.start(near[o], at(0), at(0), z_near[o])
        yield
        for o in near:
            wire.arrived(near[o], at(Z - o), z_near[o])
            if o in (3, 9):
                for hop in ((3, 2, 1) if o == 3 else (10, 11)):
                    wire.start(far[hop], at(Z - o), at(Z - o), z_near[hop])
        yield
        for o, source in ((1, 8), (11, 4), (2, 7), (10, 5), (3, 6)):
            wire.arrived(far[o], at(source), z_near[o])
        total = sums[0]
        for k in range(1, Z):
            total = total + sums[k]
        spot = weight_grad.at[me.core, me.y]
        spot[...] = total / math.sqrt(X_LO * Z * X_HI * Y * CORES * V)
        slots = [wire.slot() for _ in y_peers]
        for d, peer in enumerate(y_peers, 1):
            wire.start(slots[d - 1], spot, spot, peer)
        yield
        for d, peer in enumerate(y_peers, 1):
            wire.arrived(slots[d - 1], weight_grad.at[me.core, (me.y + Y - d) % Y], peer)
        slot = wire.slot()
        wire.start(slot, weight_grad.at[me.core], weight_grad.at[me.core], sibling)
        yield
        wire.arrived(slot, weight_grad.at[1 - me.core], sibling)

    in_turn(row_reduce(wire, me, partial, cross_buf, outgoing, relay, final, done), weight_part(),
            "ABABAABABA")
    wire.finish()


def sems(count):
    return [pltpu.SemaphoreType.DMA((count,)), pltpu.SemaphoreType.DMA((count,))]


def shape(extent, dtype):
    return jax.ShapeDtypeStruct(extent, dtype)


def talking(collective_id):
    return pltpu.CompilerParams(
        collective_id=collective_id, has_side_effects=True, vmem_limit_bytes=VMEM_BYTES)


def gather_call(count, features, scale, bits):
    return pl.pallas_call(
        gather_kernel,
        out_shape=(shape((X_LO * Z, V, V), BF16), shape((bits.shape[0], 2 * V, 2 * V), BF16)),
        in_specs=[SCALARS] + [WHOLE] * 3,
        out_specs=(WHOLE,) * 2,
        scratch_shapes=sems(24),
        compiler_params=talking(0),
        name="gather_rows",
    )(count, features, scale, bits)


def forward_call(rows, cols, count, source, masks):
    return pl.pallas_call(
        forward_kernel,
        out_shape=shape((CORES, Y, X_HI, V, V), BF16),
        in_specs=[SCALARS] * 3 + [WHOLE] * 2,
        out_specs=WHOLE,
        scratch_shapes=[pltpu.VMEM((X_HI * Y, 2 * V, V), F32)],
        compiler_params=pltpu.CompilerParams(vmem_limit_bytes=VMEM_BYTES),
        name="forward_tiles",
    )(rows, cols, count, source, masks)


def vertex_call(partial, scale, weight, cotangent):
    return pl.pallas_call(
        vertex_kernel,
        out_shape=(shape((V, 2 * V), BF16), shape((CORES, Y, X_HI, V, V), BF16), shape((8, 2 * V), F32)),
        in_specs=[WHOLE] * 4,
        out_specs=(WHOLE,) * 3,
        scratch_shapes=[
            pltpu.VMEM((Y, X_HI, V, V), BF16),
            pltpu.VMEM((Y, V, V), BF16),
            pltpu.VMEM((Y, V, V), BF16),
            pltpu.VMEM((Y, V, V), BF16),
            pltpu.VMEM((Y + 2, V, V), BF16),
            pltpu.VMEM((V, V), F32),
            pltpu.VMEM((2, V // 2, 2 * V), F32),
            pltpu.VMEM((V // 2, 2 * V), F32),
            pltpu.VMEM((Y, 8, 2 * V), F32),
            pltpu.VMEM((Y, 8, 2 * V), F32),
            pltpu.VMEM((X_LO * X_HI, 8, 2 * V), F32),
        ] + sems(72),
        compiler_params=talking(1),
        name="vertex_part",
    )(partial, scale, weight, cotangent)


def backward_call(rows, cols, count, source, masks, act):
    return pl.pallas_call(
        backward_kernel,
        out_shape=(shape((X_LO * Z, V, V), BF16), shape(act.shape, act.dtype)),
        in_specs=[SCALARS] * 3 + [WHOLE] * 3,
        out_specs=(WHOLE,) * 2,
        scratch_shapes=[pltpu.VMEM((X_LO * Z // 2, V, 2 * V), F32)],
        compiler_params=pltpu.CompilerParams(vmem_limit_bytes=VMEM_BYTES),
        name="backward_tiles",
    )(rows, cols, count, source, masks, act)


def scatter_call(partial, scale, piece):
    return pl.pallas_call(
        scatter_kernel,
        out_shape=(shape((V, V), BF16), shape((CORES, Y, 8, 2 * V), F32)),
        in_specs=[WHOLE] * 3,
        out_specs=(WHOLE,) * 2,
        scratch_shapes=[
            pltpu.VMEM((Z, V, V), BF16),
            pltpu.VMEM((Z, V, V), BF16),
            pltpu.VMEM((8, V, V), BF16),
            pltpu.VMEM((6, V, V), BF16),
            pltpu.VMEM((Z, 8, 2 * V), F32),
        ] + sems(48),
        compiler_params=talking(2),
        name="scatter_rows",
    )(partial, scale, piece)


def on_device(features, deg_scale, weight, cotangent, tile_rows, tile_cols, tile_count, tile_bits):
    rows, cols, count, bits = tile_rows[0, 0], tile_cols[0, 0], tile_count[0], tile_bits[0, 0]
    scale = deg_scale.reshape(1, V)
    column_block, masks = gather_call(count, features, scale, bits)
    partial = forward_call(rows, cols, count, column_block.reshape(Z, 2 * V, V), masks)
    act, row_block, piece = vertex_call(partial, scale, weight, cotangent)
    partial_back, activations = backward_call(rows, cols, count, row_block, masks, act)
    input_grad, grad = scatter_call(partial_back, scale, piece)
    weight_grad = grad.reshape(V, 2 * V)
    return (activations, input_grad, weight_grad)


def solution(mesh):
    in_specs = (
        P(("row", "col"), None),
        P(("row", "col")),
        P(),
        P(("row", "col"), None),
        P("row", "col", None),
        P("row", "col", None),
        P("row", "col"),
        P("row", "col", None, None, None),
    )
    out_specs = (P(("row", "col"), None), P(("row", "col"), None), P())
    return jax.shard_map(
        on_device, mesh=mesh, in_specs=in_specs, out_specs=out_specs, check_vma=False)
```
